32 devices in a mesh: req: 8 (over z, y), mlp: 4 (over x, core).
Axes of the slice: x: 2, y: 2, z: 4, core: 2. Of those that a mesh axis runs over, the one named last changes fastest.
Arguments:
- queries: bfloat16 [1024, 5120], P('req', 'mlp'), may hold values from -6 to 6
- leaf_keys: bfloat16 [1024, 1024], P('req', 'mlp'), may hold values from -6 to 6
- leaf_token_values: bfloat16 [1024, 1024], P('req', 'mlp'), may hold values from -6 to 6
- key_value_pages: bfloat16 [256, 64, 2, 1024], P('req', None, None, 'mlp'), may hold values from -6 to 6
- page_holder: int32 [8, 6, 4], replicated, may hold values from 0 to 7, as said below
- page_slot: int32 [8, 6, 4], replicated, may hold values from 0 to 31
- segment_ids: int32 [1024], P('req'), may hold values from 0 to 7, as said below
- req_parent: int32 [8, 8], P('req'), may hold values from 0 to 3
- mid_parent: int32 [8, 4], P('req'), may hold values from 0 to 1
- node_len: int32 [8, 6], P('req'), may hold values from 1 to 256
- residual: bfloat16 [1024, 5120], P('req'), may hold values from -6 to 6
- out_proj: bfloat16 [5120, 5120], P('mlp'), may hold values from -0.078125 to 0.078125
- norm_gain: float32 [5120], replicated, may hold values from 0.5 to 1.5
- gate_proj: bfloat16 [5120, 13824], P(None, ('req', 'mlp')), may hold values from -0.078125 to 0.078125
- up_proj: bfloat16 [5120, 13824], P(None, ('req', 'mlp')), may hold values from -0.078125 to 0.078125
- down_proj: bfloat16 [13824, 5120], P(('req', 'mlp')), may hold values from -0.0546875 to 0.0546875
- next_gain: float32 [5120], replicated, may hold values from 0.5 to 1.5
- qkv_proj: bfloat16 [5120, 7168], P(None, 'mlp'), may hold values from -0.078125 to 0.078125
- qkv_bias: float32 [7168], P('mlp'), may hold values from -3 to 3
Outputs:
- layer_out: bfloat16 [1024, 5120], P(('req', 'mlp'))
- qkv_out: bfloat16 [1024, 7168], P('req', 'mlp')
The draws below stay inside these ranges and needn't reach their ends.
Inputs may be any that keep to these rules, and one draw needn't show every extreme that they name: `segment_ids`: within each block of 128 tokens of one group the ids never fall, start at 0, and every id 0 to 7 occurs. `page_holder`: in each row (one group's prefix pages) exactly half of the entries name the row's own group; the other entries name other groups, no group more than 2 times in a row, and some group exactly 2 times.
All inputs are finite; a program needn't handle non-finite values.
Results may differ from the reference program's by a relative error of at most 0.02.
Values may be sent and summed in bfloat16 or wider, within the bound.
No kernel may reach another device: no remote copies, remote signals or barrier semaphores. Data moves between devices by JAX's collectives and lax.ppermute only.
A program may use at most 192 MiB of HBM per device.

```python
import math
import jax
import jax.numpy as jnp
from jax import lax

D = 5120
QUERY_HEADS = 40
KEY_VALUE_HEADS = 8
HEAD_SIZE = 128
FF = 13824
QUERY_PER_KV = 5
QKV = 7168
TOK_GRP = 128
REQ_DEV = 8
ROOT_DEV = 2
MID_DEV = 4
NODES_DEV = 6
PAGE_TOKENS = 64
NODE_PAGES = 4
NODE_MAX = 256
PAGES_PER_GROUP = 32
QUERY_TOKENS = 1024
N_REQ = 8


def segment_table(key):
    base_offset = jax.random.fold_in(key, 11)

    def one_row(row):
        order = jax.random.permutation(jax.random.fold_in(base_offset, row), TOK_GRP - 1) + 1
        marks = jnp.zeros((TOK_GRP,), jnp.int32).at[order[:REQ_DEV - 1]].set(1)
        return jnp.cumsum(marks).astype(jnp.int32)
    return jax.vmap(one_row)(jnp.arange(N_REQ)).reshape(-1)


def draw_segment_ids(key, part):
    return segment_table(key)


def draw_queries(key, part):
    token_count = N_REQ * TOK_GRP
    base_offset = jnp.clip(jax.random.normal(jax.random.fold_in(key, 32), (token_count, QUERY_HEADS * HEAD_SIZE)), -5.5, 5.5)
    return base_offset.astype(jnp.bfloat16)


def draw_leaf_keys(key, part):
    token_count = N_REQ * TOK_GRP
    base_offset = jnp.clip(jax.random.normal(jax.random.fold_in(key, 42), (token_count, KEY_VALUE_HEADS * HEAD_SIZE)), -5.5, 5.5)
    return base_offset.astype(jnp.bfloat16)


def draw_page_holder(key, part):
    base_offset = jax.random.fold_in(key, 21)
    token_count = NODES_DEV * NODE_PAGES
    half = token_count // 2

    def one_row(row):
        inner = jax.random.fold_in(base_offset, row)
        rank = jax.random.permutation(jax.random.fold_in(inner, 1), token_count)
        offsets = jax.random.permutation(jax.random.fold_in(inner, 2), N_REQ - 1)
        which = jnp.remainder(jnp.maximum(rank - half, 0), N_REQ - 1)
        distant = jnp.remainder(row + 1 + offsets[which], N_REQ)
        return jnp.where(rank < half, row, distant).astype(jnp.int32)
    return jax.vmap(one_row)(jnp.arange(N_REQ)).reshape(N_REQ, NODES_DEV, NODE_PAGES)


def place_ends(result, key, smallest, largest):
    longest = result.shape.index(max(result.shape))
    spots = []
    for shift in (0, 1):
        where = [jax.random.randint(jax.random.fold_in(key, axis), (), 0, length) for axis, length in enumerate(result.shape)]
        where[longest] = (where[longest] + shift) % result.shape[longest]
        spots.append(tuple(where))
    return result.at[spots[0]].set(smallest).at[spots[1]].set(largest)


def levels(rng, shape, split, smallest, largest):
    level = 1.0
    for axis_at, blocks in split:
        steps = jax.random.uniform(jax.random.fold_in(jax.random.fold_in(rng, 6), axis_at), (blocks,), jnp.float32, smallest / len(split), largest / len(split))
        level = level * jnp.repeat(jnp.exp(steps), shape[axis_at] // blocks).reshape((-1,) + (1,) * (len(shape) - 1 - axis_at))
    return level


def bell_draw(own_key, extent, scale, reach, split=(), held_as=jnp.bfloat16):
    drawn = scale * jax.random.normal(own_key, extent, jnp.float32)
    if split:
        drawn = drawn * levels(own_key, extent, split, -0.22, 0.18)
    return jnp.clip(drawn, -reach, reach).astype(held_as)


def setup_inputs(seed: int = 0) -> dict:
    splits = jax.random.split(jax.random.key(seed), 20)
    return {
        "queries": draw_queries(jax.random.fold_in(splits[19], 71), 0),
        "leaf_keys": draw_leaf_keys(jax.random.fold_in(splits[19], 71), 0),
        "leaf_token_values": bell_draw(splits[2], (QUERY_TOKENS, KEY_VALUE_HEADS * HEAD_SIZE), 1.0, 6.0, ((0, 8), (1, 4))),
        "key_value_pages": bell_draw(splits[3], (N_REQ * PAGES_PER_GROUP, PAGE_TOKENS, 2, KEY_VALUE_HEADS * HEAD_SIZE), 1.0, 6.0, ((0, 8), (3, 4))),
        "page_holder": draw_page_holder(jax.random.fold_in(splits[19], 71), 0),
        "page_slot": place_ends(jax.random.randint(splits[5], (N_REQ, NODES_DEV, NODE_PAGES), 0, PAGES_PER_GROUP), jax.random.fold_in(splits[5], 1), 0, PAGES_PER_GROUP - 1).astype(jnp.int32),
        "segment_ids": draw_segment_ids(jax.random.fold_in(splits[19], 71), 0),
        "req_parent": place_ends(jax.random.randint(splits[7], (N_REQ, REQ_DEV), 0, MID_DEV), jax.random.fold_in(splits[7], 1), 0, MID_DEV - 1).astype(jnp.int32),
        "mid_parent": place_ends(jax.random.randint(splits[8], (N_REQ, MID_DEV), 0, ROOT_DEV), jax.random.fold_in(splits[8], 1), 0, ROOT_DEV - 1).astype(jnp.int32),
        "node_len": place_ends(jax.random.randint(splits[9], (N_REQ, NODES_DEV), 1, NODE_MAX + 1), jax.random.fold_in(splits[9], 1), 1, NODE_MAX).astype(jnp.int32),
        "residual": bell_draw(splits[10], (QUERY_TOKENS, D), 1.0, 6.0, ((0, 8),)),
        "out_proj": bell_draw(splits[11], (QUERY_HEADS * HEAD_SIZE, D), (QUERY_HEADS * HEAD_SIZE) ** -0.5, 0.078125, ((0, 4),)),
        "norm_gain": jnp.clip(1.0 + 0.1 * jax.random.normal(splits[12], (D,), jnp.float32), 0.5, 1.5),
        "gate_proj": bell_draw(splits[13], (D, FF), D ** -0.5, 0.078125, ((1, 32),)),
        "up_proj": bell_draw(splits[14], (D, FF), D ** -0.5, 0.078125, ((1, 32),)),
        "down_proj": bell_draw(splits[15], (FF, D), FF ** -0.5, 0.0546875, ((0, 32),)),
        "next_gain": jnp.clip(1.0 + 0.1 * jax.random.normal(splits[16], (D,), jnp.float32), 0.5, 1.5),
        "qkv_proj": bell_draw(splits[17], (D, QKV), D ** -0.5, 0.078125, ((1, 4),)),
        "qkv_bias": bell_draw(splits[18], (QKV,), 0.5, 3.0, ((0, 4),), jnp.float32),
    }


EPS = 1e-06

def rms_norm(stream, gain):
    values = stream.astype(jnp.float32)
    mean_sq = lax.optimization_barrier(jnp.mean(values * values, axis=-1, keepdims=True))
    return (values * lax.rsqrt(mean_sq + EPS) * gain).astype(jnp.bfloat16)

def attend(queries, leaf_keys, leaf_token_values, prefix_keys, prefix_values, segments, parents, roots, lengths):
    tokens = queries.shape[0]
    heads_kv = leaf_keys.shape[1] // HEAD_SIZE
    query_rows = queries.reshape(tokens, heads_kv, QUERY_PER_KV, HEAD_SIZE).astype(jnp.float32)
    keys = jnp.concatenate([prefix_keys.reshape(-1, heads_kv, HEAD_SIZE), leaf_keys.reshape(tokens, heads_kv, HEAD_SIZE)], 0)
    values = jnp.concatenate([prefix_values.reshape(-1, heads_kv, HEAD_SIZE), leaf_token_values.reshape(tokens, heads_kv, HEAD_SIZE)], 0)
    middle = lax.optimization_barrier(jnp.sum((segments[:, None] == jnp.arange(REQ_DEV)[None, :]) * parents[None, :], axis=1))
    root = lax.optimization_barrier(jnp.sum((middle[:, None] == jnp.arange(MID_DEV)[None, :]) * roots[None, :], axis=1))
    node = jnp.arange(NODES_DEV * NODE_MAX) // NODE_MAX
    inside = (jnp.arange(NODE_MAX)[None, :] < lengths[:, None]).reshape(-1)
    prefix_mask = ((node[None, :] == root[:, None]) | (node[None, :] == ROOT_DEV + middle[:, None])) & inside[None, :]
    place = jnp.arange(tokens)
    leaf_mask = (segments[None, :] == segments[:, None]) & (place[None, :] <= place[:, None])
    mask = jnp.concatenate([prefix_mask, leaf_mask], 1)
    score = jnp.einsum('tkgd,skd->tkgs', query_rows, keys.astype(jnp.float32)) / math.sqrt(HEAD_SIZE)
    score = jnp.where(mask[:, None, None, :], score, -1e+30)
    top = lax.optimization_barrier(jnp.max(score, axis=-1, keepdims=True))
    expo = jnp.where(mask[:, None, None, :], jnp.exp(score - top), 0.0)
    total = lax.optimization_barrier(jnp.sum(expo, axis=-1, keepdims=True))
    weights = expo.astype(jnp.bfloat16)
    summed = jnp.einsum('tkgs,skd->tkgd', weights.astype(jnp.float32), values.astype(jnp.float32))
    return (summed / total).astype(jnp.bfloat16).reshape(tokens, -1)

def reference(queries, leaf_keys, leaf_token_values, key_value_pages, page_holder, page_slot, segment_ids, req_parent, mid_parent, node_len, residual, out_proj, norm_gain, gate_proj, up_proj, down_proj, next_gain, qkv_proj, qkv_bias):
    index = (page_holder * PAGES_PER_GROUP + page_slot).astype(jnp.int32)

    def one_group(group):
        pages = key_value_pages[index[group].reshape(-1)]
        prefix = pages.reshape(NODES_DEV * NODE_MAX, 2, -1)
        start = (group * TOK_GRP).astype(jnp.int32)
        return attend(lax.dynamic_slice_in_dim(queries, start, TOK_GRP, 0), lax.dynamic_slice_in_dim(leaf_keys, start, TOK_GRP, 0), lax.dynamic_slice_in_dim(leaf_token_values, start, TOK_GRP, 0), prefix[:, 0], prefix[:, 1], lax.dynamic_slice_in_dim(segment_ids, start, TOK_GRP, 0), req_parent[group], mid_parent[group], node_len[group])
    attention = lax.map(one_group, jnp.arange(N_REQ, dtype=jnp.int32)).reshape(QUERY_TOKENS, -1)
    projected = jnp.dot(attention, out_proj, preferred_element_type=jnp.float32)
    stream = (residual.astype(jnp.float32) + projected).astype(jnp.bfloat16)
    normed = rms_norm(stream, norm_gain)
    gate = jnp.dot(normed, gate_proj, preferred_element_type=jnp.float32)
    upper = jnp.dot(normed, up_proj, preferred_element_type=jnp.float32)
    hidden = (jax.nn.silu(gate) * upper).astype(jnp.bfloat16)
    mixed = jnp.dot(hidden, down_proj, preferred_element_type=jnp.float32)
    layer_out = (stream.astype(jnp.float32) + mixed).astype(jnp.bfloat16)
    next_normed = rms_norm(layer_out, next_gain)
    qkv_out = (jnp.dot(next_normed, qkv_proj, preferred_element_type=jnp.float32) + qkv_bias).astype(jnp.bfloat16)
    return (layer_out, qkv_out)
```

```python
import math

import jax
import jax.numpy as jnp
from jax import lax
from jax.sharding import PartitionSpec as P

HEAD_SIZE = 128
QUERY_PER_KV = 5
REQ_DEV = 8
ROOT_DEV = 2
MID_DEV = 4
NODES_DEV = 6
NODE_MAX = 256
OUTER = 4
CHUNKS = 2


EPS = 1e-06


def rms_norm(stream, gain):
    values = stream.astype(jnp.float32)
    mean_sq = jnp.mean(values * values, axis=-1, keepdims=True)
    return (values * lax.rsqrt(mean_sq + EPS) * gain).astype(jnp.bfloat16)


def swap(array, axis, step):
    return lax.ppermute(array, axis, [(i, i ^ step) for i in range(lax.axis_size(axis))])


def attend(
    queries,
    places,
    query_segments,
    leaf_keys,
    leaf_token_values,
    prefix_keys,
    prefix_values,
    segments,
    parents,
    roots,
    lengths,
):
    tokens = queries.shape[0]
    leaf_tokens = leaf_keys.shape[0]
    heads_kv = leaf_keys.shape[1] // HEAD_SIZE
    query_rows = queries.reshape(tokens, heads_kv, QUERY_PER_KV, HEAD_SIZE)
    keys = jnp.concatenate(
        [
            prefix_keys.reshape(-1, heads_kv, HEAD_SIZE),
            leaf_keys.reshape(leaf_tokens, heads_kv, HEAD_SIZE),
        ],
        0,
    )
    values = jnp.concatenate(
        [
            prefix_values.reshape(-1, heads_kv, HEAD_SIZE),
            leaf_token_values.reshape(leaf_tokens, heads_kv, HEAD_SIZE),
        ],
        0,
    )
    middle = jnp.sum(
        (query_segments[:, None] == jnp.arange(REQ_DEV)[None, :]) * parents[None, :], axis=1
    )
    root = jnp.sum((middle[:, None] == jnp.arange(MID_DEV)[None, :]) * roots[None, :], axis=1)
    node = jnp.arange(NODES_DEV * NODE_MAX) // NODE_MAX
    inside = (jnp.arange(NODE_MAX)[None, :] < lengths[:, None]).reshape(-1)
    prefix_mask = (
        (node[None, :] == root[:, None]) | (node[None, :] == ROOT_DEV + middle[:, None])
    ) & inside[None, :]
    leaf_mask = (segments[None, :] == query_segments[:, None]) & (
        jnp.arange(leaf_tokens)[None, :] <= places[:, None]
    )
    mask = jnp.concatenate([prefix_mask, leaf_mask], 1)
    score = jnp.einsum(
        "tkgd,skd->tkgs", query_rows, keys, preferred_element_type=jnp.float32
    ) / math.sqrt(HEAD_SIZE)
    score = jnp.where(mask[:, None, None, :], score, -1e30)
    top = jnp.max(score, axis=-1, keepdims=True)
    expo = jnp.where(mask[:, None, None, :], jnp.exp(score - top), 0.0)
    total = jnp.sum(expo, axis=-1, keepdims=True)
    weights = expo.astype(jnp.bfloat16)
    summed = jnp.einsum("tkgs,skd->tkgd", weights, values, preferred_element_type=jnp.float32)
    return (summed / total).astype(jnp.bfloat16).reshape(tokens, -1)


def fetch_prefix(key_value_pages, page_holder, page_slot):
    groups = lax.axis_size("req")
    myself = lax.axis_index("req")
    holders = page_holder.reshape(groups, -1)
    slots = page_slot.reshape(groups, -1)
    token_count = holders.shape[1]
    room = (token_count // 2 + groups - 2) // (groups - 1)
    earlier = jnp.arange(token_count)[None, :] < jnp.arange(token_count)[:, None]
    same = holders[:, :, None] == holders[:, None, :]
    rank = jnp.sum(same & earlier[None, :, :], axis=-1)
    asked = (holders == myself) & (jnp.arange(groups)[:, None] != myself)
    picked = asked[:, None, :] & (rank[:, None, :] == jnp.arange(room)[None, :, None])
    send_slot = jnp.sum(jnp.where(picked, slots[:, None, :], 0), axis=-1)
    outgoing = key_value_pages[send_slot]
    incoming = lax.all_to_all(outgoing, "req", split_axis=0, concat_axis=0, tiled=True)
    flat_in = incoming.reshape((groups * room,) + incoming.shape[2:])
    own_holders = lax.dynamic_index_in_dim(holders, myself, 0, keepdims=False)
    own_slots = lax.dynamic_index_in_dim(slots, myself, 0, keepdims=False)
    own_rank = lax.dynamic_index_in_dim(rank, myself, 0, keepdims=False)
    remote = flat_in[own_holders * room + jnp.minimum(own_rank, room - 1)]
    local = key_value_pages[own_slots]
    pages = jnp.where((own_holders == myself)[:, None, None, None], local, remote)
    return pages.reshape(NODES_DEV * NODE_MAX, 2, -1)


def gather_tokens(rows):
    inner = lax.axis_size("req") // OUTER
    across = lax.axis_size("mlp") // 2
    column = jnp.concatenate(
        [rows] + [swap(rows, "req", k * inner) for k in range(1, OUTER)], 0
    )
    half = column.shape[0] // 2
    by_x = {k: swap(column, "mlp", 2 * k) for k in range(1, across)}
    by_y = {l: swap(column, "req", l) for l in range(1, inner)}
    blocks = [column] + list(by_x.values()) + list(by_y.values())
    for k in range(1, across):
        for l in range(1, inner):
            blocks.append(swap(by_y[l][:half], "mlp", 2 * k))
            blocks.append(swap(by_x[k][half:], "req", l))
    return jnp.concatenate(blocks, 0)


def scatter_sum(partial, rows):
    inner = lax.axis_size("req") // OUTER
    across = lax.axis_size("mlp") // 2
    size = OUTER * rows
    half = size // 2
    blocks = [partial[i * size : (i + 1) * size] for i in range(across * inner)]
    wide = jnp.float32
    column = blocks[0].astype(wide)
    by_x = {k: blocks[k].astype(wide) for k in range(1, across)}
    by_y = {l: blocks[across - 1 + l].astype(wide) for l in range(1, inner)}
    at = across + inner - 1
    for k in range(1, across):
        for l in range(1, inner):
            first = swap(blocks[at][:half], "mlp", 2 * k).astype(wide)
            second = swap(blocks[at][half:], "req", l).astype(wide)
            by_y[l] = jnp.concatenate([by_y[l][:half] + first, by_y[l][half:]], 0)
            by_x[k] = jnp.concatenate([by_x[k][:half], by_x[k][half:] + second], 0)
            at += 1
    for k in range(1, across):
        column = column + swap(by_x[k].astype(jnp.bfloat16), "mlp", 2 * k).astype(wide)
    for l in range(1, inner):
        column = column + swap(by_y[l].astype(jnp.bfloat16), "req", l).astype(wide)
    total = column[:rows]
    for k in range(1, OUTER):
        part = column[k * rows : (k + 1) * rows].astype(jnp.bfloat16)
        total = total + swap(part, "req", k * inner).astype(wide)
    return total


def sum_heads(projected, rows):
    members = lax.axis_size("mlp")
    wide = jnp.float32
    blocks = [projected[j * rows : (j + 1) * rows] for j in range(members)]
    odd = jnp.concatenate(blocks[1::2], 0).astype(jnp.bfloat16)
    even = jnp.concatenate(blocks[0::2], 0) + swap(odd, "mlp", 1).astype(wide)
    total = even[:rows]
    for k in range(1, members // 2):
        part = even[k * rows : (k + 1) * rows].astype(jnp.bfloat16)
        total = total + swap(part, "mlp", 2 * k).astype(wide)
    return total


def gather_heads(rows):
    members = lax.axis_size("mlp")
    place = lax.axis_index("mlp")
    blocks = [rows] + [swap(rows, "mlp", 2 * k) for k in range(1, members // 2)]
    near = jnp.concatenate(blocks, 0)
    far = swap(near, "mlp", 1)
    size = rows.shape[0]
    near = near.reshape(members // 2, size, -1)
    far = far.reshape(members // 2, size, -1)
    core = place % 2
    low = jnp.where(core == 0, near, far)
    high = jnp.where(core == 0, far, near)
    pairs = jnp.stack([low, high], 1)
    for bit in range((members // 2).bit_length() - 1):
        shaped = pairs.reshape((-1, 2, 1 << bit) + pairs.shape[1:])
        swapped = shaped[:, ::-1]
        shaped = jnp.where(((place // 2) >> bit) % 2 == 0, shaped, swapped)
        pairs = shaped.reshape(pairs.shape)
    return pairs.reshape(members, size, -1)


def body(
    queries,
    leaf_keys,
    leaf_token_values,
    key_value_pages,
    page_holder,
    page_slot,
    segment_ids,
    req_parent,
    mid_parent,
    node_len,
    residual,
    out_proj,
    norm_gain,
    gate_proj,
    up_proj,
    down_proj,
    next_gain,
    qkv_proj,
    qkv_bias,
):
    group_tokens = queries.shape[0]
    members = lax.axis_size("mlp")
    place = lax.axis_index("mlp")
    owned = group_tokens // members
    rows = owned // CHUNKS
    gates = [gate_proj, swap(gate_proj, "mlp", 1)]
    uppers = [up_proj, swap(up_proj, "mlp", 1)]
    downs = [down_proj, swap(down_proj, "mlp", 1)]
    prefix = fetch_prefix(key_value_pages, page_holder, page_slot)

    def attention_of(chunk):
        starts = [(place ^ j) * owned + chunk * rows for j in range(members)]

        def picked(array):
            return jnp.concatenate(
                [lax.dynamic_slice_in_dim(array, s, rows, 0) for s in starts], 0
            )

        places = jnp.concatenate([s + jnp.arange(rows) for s in starts], 0)
        attention = attend(
            picked(queries),
            places,
            picked(segment_ids),
            leaf_keys,
            leaf_token_values,
            prefix[:, 0],
            prefix[:, 1],
            segment_ids,
            req_parent[0],
            mid_parent[0],
            node_len[0],
        )
        return jnp.dot(attention, out_proj, preferred_element_type=jnp.float32)

    def stream_of(chunk, projected):
        own = lax.dynamic_slice_in_dim(residual, place * owned + chunk * rows, rows, 0)
        return (own.astype(jnp.float32) + sum_heads(projected, rows)).astype(jnp.bfloat16)

    def mixed_of(tokens):
        total = None
        for gate_w, up_w, down_w in zip(gates, uppers, downs):
            gate = jnp.dot(tokens, gate_w, preferred_element_type=jnp.float32)
            upper = jnp.dot(tokens, up_w, preferred_element_type=jnp.float32)
            hidden = (jax.nn.silu(gate) * upper).astype(jnp.bfloat16)
            part = jnp.dot(hidden, down_w, preferred_element_type=jnp.float32)
            total = part if total is None else total + part
        return total.astype(jnp.bfloat16)

    layer_rows, next_rows = [], []
    for chunk in range(CHUNKS):
        stream = stream_of(chunk, attention_of(chunk))
        tokens = gather_tokens(rms_norm(stream, norm_gain))
        mixed = scatter_sum(mixed_of(tokens), rows)
        layer = (stream.astype(jnp.float32) + mixed).astype(jnp.bfloat16)
        layer_rows.append(layer)
        next_rows.append(gather_heads(rms_norm(layer, next_gain)))
    layer_out = jnp.concatenate(layer_rows, 0)
    next_normed = jnp.concatenate(next_rows, 1).reshape(group_tokens, -1)
    qkv_out = (
        jnp.dot(next_normed, qkv_proj, preferred_element_type=jnp.float32) + qkv_bias
    ).astype(jnp.bfloat16)
    return (layer_out, qkv_out)


def solution(mesh):
    placed = (
        P("req", "mlp"),
        P("req", "mlp"),
        P("req", "mlp"),
        P("req", None, None, "mlp"),
        P(),
        P(),
        P("req"),
        P("req", None),
        P("req", None),
        P("req", None),
        P("req", None),
        P("mlp", None),
        P(),
        P(None, ("req", "mlp")),
        P(None, ("req", "mlp")),
        P(("req", "mlp"), None),
        P(),
        P(None, "mlp"),
        P("mlp"),
    )
    return jax.shard_map(
        body,
        mesh=mesh,
        in_specs=placed,
        out_specs=(P(("req", "mlp"), None), P("req", "mlp")),
        check_vma=False,
    )
```

```python
import math

import jax
import jax.numpy as jnp
from jax import lax
from jax.experimental import pallas as pl
from jax.experimental.pallas import tpu as pltpu
from jax.sharding import PartitionSpec as P

HEAD_SIZE = 128
QUERY_PER_KV = 5
REQ_DEV = 8
ROOT_DEV = 2
MID_DEV = 4
NODES_DEV = 6
NODE_MAX = 256
OUTER = 4
CHUNKS = 2


EPS = 1e-06


def rms_norm(stream, gain):
    values = stream.astype(jnp.float32)
    mean_sq = jnp.mean(values * values, axis=-1, keepdims=True)
    return (values * lax.rsqrt(mean_sq + EPS) * gain).astype(jnp.bfloat16)


def swap(array, axis, step):
    return lax.ppermute(array, axis, [(i, i ^ step) for i in range(lax.axis_size(axis))])


def attend_kernel(
    local_ref,
    entry_ref,
    queries_ref,
    limits_ref,
    query_segments_ref,
    places_ref,
    segments_ref,
    own_pages_ref,
    sent_pages_ref,
    leaf_keys_ref,
    leaf_values_ref,
    out_ref,
    keys,
    values,
    mask,
):
    tokens = queries_ref.shape[0]
    page = own_pages_ref.shape[2]
    pages = own_pages_ref.shape[0]
    prefix = pages * page
    node_tokens = prefix // NODES_DEV
    leaf_tokens = leaf_keys_ref.shape[0]
    heads_kv = leaf_keys_ref.shape[1] // HEAD_SIZE
    for p in range(pages):
        span = pl.ds(p * page, page)

        @pl.when(local_ref[p] == 1)
        def _():
            keys[span] = own_pages_ref[p, 0]
            values[span] = own_pages_ref[p, 1]

        @pl.when(local_ref[p] == 0)
        def _():
            keys[span] = sent_pages_ref[entry_ref[p], 0]
            values[span] = sent_pages_ref[entry_ref[p], 1]

    keys[pl.ds(prefix, leaf_tokens)] = leaf_keys_ref[...]
    values[pl.ds(prefix, leaf_tokens)] = leaf_values_ref[...]
    at = lax.broadcasted_iota(jnp.int32, (tokens, node_tokens), 1)
    for n in range(NODES_DEV):
        seen = at < limits_ref[:, n : n + 1]
        mask[:, n * node_tokens : (n + 1) * node_tokens] = jnp.where(seen, 0.0, -1e30)
    at = lax.broadcasted_iota(jnp.int32, (tokens, leaf_tokens), 1)
    seen = (segments_ref[...] == query_segments_ref[...]) & (at <= places_ref[...])
    mask[:, prefix:] = jnp.where(seen, 0.0, -1e30)
    scale = 1.0 / math.sqrt(HEAD_SIZE)
    for h in range(heads_kv * QUERY_PER_KV):
        group = pl.ds(h // QUERY_PER_KV * HEAD_SIZE, HEAD_SIZE)
        head = pl.ds(h * HEAD_SIZE, HEAD_SIZE)
        score = lax.dot_general(
            queries_ref[:, head],
            keys[:, group],
            (((1,), (1,)), ((), ())),
            preferred_element_type=jnp.float32,
        )
        score = score * scale + mask[...]
        top = jnp.max(score, axis=1, keepdims=True)
        expo = jnp.exp(score - top)
        total = jnp.sum(expo, axis=1, keepdims=True)
        summed = jnp.dot(
            expo.astype(jnp.bfloat16), values[:, group], preferred_element_type=jnp.float32
        )
        out_ref[:, head] = (summed / total).astype(jnp.bfloat16)


def attend(
    queries, places, query_segments, leaf_keys, leaf_values, fetched, segments, parents, roots, lengths
):
    is_local, entry, own_pages, sent_pages = fetched
    tokens, leaf_tokens = queries.shape[0], leaf_keys.shape[0]
    middle = jnp.sum(
        (query_segments[:, None] == jnp.arange(REQ_DEV)[None, :]) * parents[None, :], axis=1
    )
    root = jnp.sum((middle[:, None] == jnp.arange(MID_DEV)[None, :]) * roots[None, :], axis=1)
    node = jnp.arange(NODES_DEV)[None, :]
    on_path = (node == root[:, None]) | (node == ROOT_DEV + middle[:, None])
    limits = jnp.where(on_path, lengths[None, :], 0)
    key_count = NODES_DEV * NODE_MAX + leaf_tokens
    scalars = pl.BlockSpec(memory_space=pltpu.SMEM)
    whole = pl.BlockSpec(memory_space=pltpu.VMEM)
    columns = leaf_keys.shape[1]
    heads = queries.shape[1] // HEAD_SIZE
    return pl.pallas_call(
        attend_kernel,
        in_specs=[scalars] * 2 + [whole] * 9,
        out_specs=whole,
        out_shape=jax.ShapeDtypeStruct(queries.shape, jnp.bfloat16),
        scratch_shapes=[
            pltpu.VMEM((key_count, columns), jnp.bfloat16),
            pltpu.VMEM((key_count, columns), jnp.bfloat16),
            pltpu.VMEM((tokens, key_count), jnp.float32),
        ],
        compiler_params=pltpu.CompilerParams(vmem_limit_bytes=20 * 1024 * 1024),
        cost_estimate=pl.CostEstimate(
            flops=4 * tokens * heads * HEAD_SIZE * key_count,
            bytes_accessed=8 * key_count * columns,
            transcendentals=tokens * heads * key_count,
        ),
        name="attend",
    )(
        is_local,
        entry,
        queries,
        limits,
        query_segments[:, None],
        places[:, None],
        segments[None, :],
        own_pages,
        sent_pages,
        leaf_keys,
        leaf_values,
    )


def fetch_prefix(key_value_pages, page_holder, page_slot):
    groups = lax.axis_size("req")
    myself = lax.axis_index("req")
    holders = page_holder.reshape(groups, -1)
    slots = page_slot.reshape(groups, -1)
    token_count = holders.shape[1]
    room = (token_count // 2 + groups - 2) // (groups - 1)
    earlier = jnp.arange(token_count)[None, :] < jnp.arange(token_count)[:, None]
    same = holders[:, :, None] == holders[:, None, :]
    rank = jnp.sum(same & earlier[None, :, :], axis=-1)
    asked = (holders == myself) & (jnp.arange(groups)[:, None] != myself)
    picked = asked[:, None, :] & (rank[:, None, :] == jnp.arange(room)[None, :, None])
    send_slot = jnp.sum(jnp.where(picked, slots[:, None, :], 0), axis=-1)
    outgoing = jnp.swapaxes(key_value_pages[send_slot.reshape(-1)], 1, 2)
    incoming = lax.all_to_all(outgoing, "req", split_axis=0, concat_axis=0, tiled=True)
    own_holders = lax.dynamic_index_in_dim(holders, myself, 0, keepdims=False)
    own_slots = lax.dynamic_index_in_dim(slots, myself, 0, keepdims=False)
    own_rank = lax.dynamic_index_in_dim(rank, myself, 0, keepdims=False)
    entry = own_holders * room + jnp.minimum(own_rank, room - 1)
    local = jnp.swapaxes(key_value_pages[own_slots], 1, 2)
    return (own_holders == myself).astype(jnp.int32), entry, local, incoming


def gather_tokens(rows):
    inner = lax.axis_size("req") // OUTER
    across = lax.axis_size("mlp") // 2
    column = jnp.concatenate(
        [rows] + [swap(rows, "req", k * inner) for k in range(1, OUTER)], 0
    )
    half = column.shape[0] // 2
    by_x = {k: swap(column, "mlp", 2 * k) for k in range(1, across)}
    by_y = {l: swap(column, "req", l) for l in range(1, inner)}
    blocks = [column] + list(by_x.values()) + list(by_y.values())
    for k in range(1, across):
        for l in range(1, inner):
            blocks.append(swap(by_y[l][:half], "mlp", 2 * k))
            blocks.append(swap(by_x[k][half:], "req", l))
    return jnp.concatenate(blocks, 0)


def scatter_sum(partial, rows):
    inner = lax.axis_size("req") // OUTER
    across = lax.axis_size("mlp") // 2
    size = OUTER * rows
    half = size // 2
    blocks = [partial[i * size : (i + 1) * size] for i in range(across * inner)]
    wide = jnp.float32
    column = blocks[0].astype(wide)
    by_x = {k: blocks[k].astype(wide) for k in range(1, across)}
    by_y = {l: blocks[across - 1 + l].astype(wide) for l in range(1, inner)}
    at = across + inner - 1
    for k in range(1, across):
        for l in range(1, inner):
            first = swap(blocks[at][:half], "mlp", 2 * k).astype(wide)
            second = swap(blocks[at][half:], "req", l).astype(wide)
            by_y[l] = jnp.concatenate([by_y[l][:half] + first, by_y[l][half:]], 0)
            by_x[k] = jnp.concatenate([by_x[k][:half], by_x[k][half:] + second], 0)
            at += 1
    for k in range(1, across):
        column = column + swap(by_x[k].astype(jnp.bfloat16), "mlp", 2 * k).astype(wide)
    for l in range(1, inner):
        column = column + swap(by_y[l].astype(jnp.bfloat16), "req", l).astype(wide)
    total = column[:rows]
    for k in range(1, OUTER):
        part = column[k * rows : (k + 1) * rows].astype(jnp.bfloat16)
        total = total + swap(part, "req", k * inner).astype(wide)
    return total


def sum_cores(projected, rows):
    members = lax.axis_size("mlp")
    wide = jnp.float32
    blocks = [projected[j * rows : (j + 1) * rows] for j in range(members)]
    odd = jnp.concatenate(blocks[1::2], 0).astype(jnp.bfloat16)
    return jnp.concatenate(blocks[0::2], 0) + swap(odd, "mlp", 1).astype(wide)


def sum_across(even, rows):
    members = lax.axis_size("mlp")
    wide = jnp.float32
    total = even[:rows]
    for k in range(1, members // 2):
        part = even[k * rows : (k + 1) * rows].astype(jnp.bfloat16)
        total = total + swap(part, "mlp", 2 * k).astype(wide)
    return total


def gather_heads(rows):
    members = lax.axis_size("mlp")
    place = lax.axis_index("mlp")
    size = rows.shape[0]
    near = [rows] + [swap(rows, "mlp", 2 * k) for k in range(1, members // 2)]
    far = swap(jnp.concatenate(near, 0), "mlp", 1)
    blocks = []
    for k, block in enumerate(near):
        blocks += [block, far[k * size : (k + 1) * size]]
    step = 1
    while step < members:
        flip = (place // step) % 2 == 1
        blocks = [
            jnp.where(flip, blocks[j ^ step], blocks[j]) for j in range(members)
        ]
        step *= 2
    return blocks


def feed_forward_kernel(
    steps_in, x_ref, g0_ref, g1_ref, u0_ref, u1_ref, d0_ref, d1_ref, out_ref, acc, hidden
):
    step = pl.program_id(0)
    wide = jnp.float32

    @pl.when(step < steps_in)
    def _():
        x = x_ref[...]
        parts = [
            lax.dot_general(x, w[...], (((1,), (1,)), ((), ())), preferred_element_type=wide)
            for w in (g0_ref, g1_ref, u0_ref, u1_ref)
        ]

        @pl.when(step == 0)
        def _():
            for n, part in enumerate(parts):
                acc[n] = part

        @pl.when(step > 0)
        def _():
            for n, part in enumerate(parts):
                acc[n] += part

    @pl.when(step == steps_in - 1)
    def _():
        for n in range(2):
            gate = acc[n]
            hidden[n] = (gate / (1.0 + jnp.exp(-gate)) * acc[2 + n]).astype(jnp.bfloat16)

    @pl.when(step >= steps_in)
    def _():
        total = jnp.dot(hidden[0], d0_ref[...], preferred_element_type=wide)
        total += jnp.dot(hidden[1], d1_ref[...], preferred_element_type=wide)
        out_ref[...] = total.astype(jnp.bfloat16)


def feed_forward(tokens, gates, uppers, downs):
    rows, width = tokens.shape
    units = gates[0].shape[0]
    steps_in, steps_out = 4, 4
    depth, span = width // steps_in, width // steps_out

    def inner(i):
        return jnp.minimum(i, steps_in - 1)

    def outer(i):
        return jnp.maximum(i - steps_in, 0)

    weight = pl.BlockSpec((units, depth), lambda i: (0, inner(i)))
    down = pl.BlockSpec((units, span), lambda i: (0, outer(i)))
    return pl.pallas_call(
        lambda *refs: feed_forward_kernel(steps_in, *refs),
        grid=(steps_in + steps_out,),
        in_specs=[pl.BlockSpec((rows, depth), lambda i: (0, inner(i)))]
        + [weight] * 4
        + [down] * 2,
        out_specs=pl.BlockSpec((rows, span), lambda i: (0, outer(i))),
        out_shape=jax.ShapeDtypeStruct((rows, width), jnp.bfloat16),
        scratch_shapes=[
            pltpu.VMEM((4, rows, units), jnp.float32),
            pltpu.VMEM((2, rows, units), jnp.bfloat16),
        ],
        compiler_params=pltpu.CompilerParams(vmem_limit_bytes=24 * 1024 * 1024),
        cost_estimate=pl.CostEstimate(
            flops=12 * rows * width * units,
            bytes_accessed=12 * width * units + 4 * rows * width,
            transcendentals=2 * rows * units,
        ),
        name="feed_forward",
    )(tokens, *gates, *uppers, *downs)


def body(
    queries,
    leaf_keys,
    leaf_token_values,
    key_value_pages,
    page_holder,
    page_slot,
    segment_ids,
    req_parent,
    mid_parent,
    node_len,
    residual,
    out_proj,
    norm_gain,
    gate_proj,
    up_proj,
    down_proj,
    next_gain,
    qkv_proj,
    qkv_bias,
):
    group_tokens = queries.shape[0]
    members = lax.axis_size("mlp")
    place = lax.axis_index("mlp")
    owned = group_tokens // members
    rows = owned // CHUNKS
    gate_rows, up_rows = gate_proj.T, up_proj.T
    gates = [gate_rows, swap(gate_rows, "mlp", 1)]
    uppers = [up_rows, swap(up_rows, "mlp", 1)]
    downs = [down_proj, swap(down_proj, "mlp", 1)]
    fetched = fetch_prefix(key_value_pages, page_holder, page_slot)
    starts = [
        (place ^ j) * owned + chunk * rows for chunk in range(CHUNKS) for j in range(members)
    ]

    def picked(array):
        return jnp.concatenate([lax.dynamic_slice_in_dim(array, s, rows, 0) for s in starts], 0)

    places = jnp.concatenate([s + jnp.arange(rows) for s in starts], 0)
    asked, fetched, gates, uppers, downs = lax.optimization_barrier(
        (picked(queries), fetched, gates, uppers, downs)
    )
    attention = attend(
        asked,
        places,
        picked(segment_ids),
        leaf_keys,
        leaf_token_values,
        fetched,
        segment_ids,
        req_parent[0],
        mid_parent[0],
        node_len[0],
    )
    projected = jnp.dot(attention, out_proj, preferred_element_type=jnp.float32)
    span = members * rows
    evens = [sum_cores(projected[c * span : (c + 1) * span], rows) for c in range(CHUNKS)]
    streams, mixed = [], []
    for chunk in range(CHUNKS):
        own = lax.dynamic_slice_in_dim(residual, place * owned + chunk * rows, rows, 0)
        summed = sum_across(evens[chunk], rows)
        streams.append((own.astype(jnp.float32) + summed).astype(jnp.bfloat16))
    for chunk in range(CHUNKS):
        tokens = gather_tokens(rms_norm(streams[chunk], norm_gain))
        mixed.append(feed_forward(tokens, gates, uppers, downs))
    layer_rows, next_rows = [], []
    for chunk in range(CHUNKS):
        summed = scatter_sum(mixed[chunk], rows)
        layer = (streams[chunk].astype(jnp.float32) + summed).astype(jnp.bfloat16)
        layer_rows.append(layer)
        next_rows.append(gather_heads(rms_norm(layer, next_gain)))
    layer_out = jnp.concatenate(layer_rows, 0)
    next_normed = jnp.concatenate(
        [next_rows[c][j] for j in range(members) for c in range(CHUNKS)], 0
    )
    qkv_out = (
        jnp.dot(next_normed, qkv_proj, preferred_element_type=jnp.float32) + qkv_bias
    ).astype(jnp.bfloat16)
    return (layer_out, qkv_out)


def solution(mesh):
    placed = (
        P("req", "mlp"),
        P("req", "mlp"),
        P("req", "mlp"),
        P("req", None, None, "mlp"),
        P(),
        P(),
        P("req"),
        P("req", None),
        P("req", None),
        P("req", None),
        P("req", None),
        P("mlp", None),
        P(),
        P(None, ("req", "mlp")),
        P(None, ("req", "mlp")),
        P(("req", "mlp"), None),
        P(),
        P(None, "mlp"),
        P("mlp"),
    )
    return jax.shard_map(
        body,
        mesh=mesh,
        in_specs=placed,
        out_specs=(P(("req", "mlp"), None), P("req", "mlp")),
        check_vma=False,
    )
```

```python
import math

import jax
import jax.numpy as jnp
from jax import lax
from jax.experimental import pallas as pl
from jax.experimental.pallas import tpu as pltpu
from jax.sharding import PartitionSpec as P

HEAD_SIZE = 128
QUERY_PER_KV = 5
REQ_DEV = 8
ROOT_DEV = 2
MID_DEV = 4
NODES_DEV = 6
NODE_MAX = 256
OUTER = 4
CHUNKS = 2


EPS = 1e-06


def rms_norm(stream, gain):
    values = stream.astype(jnp.float32)
    mean_sq = jnp.mean(values * values, axis=-1, keepdims=True)
    return (values * lax.rsqrt(mean_sq + EPS) * gain).astype(jnp.bfloat16)


def swap(array, axis, step):
    return lax.ppermute(array, axis, [(i, i ^ step) for i in range(lax.axis_size(axis))])


def attend_kernel(
    local_ref,
    entry_ref,
    queries_ref,
    limits_ref,
    query_segments_ref,
    places_ref,
    segments_ref,
    own_pages_ref,
    sent_pages_ref,
    leaf_keys_ref,
    leaf_values_ref,
    proj_ref,
    out_ref,
    keys,
    values,
    mask,
    heads_out,
    proj,
    proj_sem,
):
    fetch = pltpu.make_async_copy(proj_ref, proj, proj_sem)
    fetch.start()
    tokens = queries_ref.shape[0]
    page = own_pages_ref.shape[2]
    pages = own_pages_ref.shape[0]
    prefix = pages * page
    node_tokens = prefix // NODES_DEV
    leaf_tokens = leaf_keys_ref.shape[0]
    heads_kv = leaf_keys_ref.shape[1] // HEAD_SIZE
    for p in range(pages):
        span = pl.ds(p * page, page)

        @pl.when(local_ref[p] == 1)
        def _():
            keys[span] = own_pages_ref[p, 0]
            values[span] = own_pages_ref[p, 1]

        @pl.when(local_ref[p] == 0)
        def _():
            keys[span] = sent_pages_ref[entry_ref[p], 0]
            values[span] = sent_pages_ref[entry_ref[p], 1]

    keys[pl.ds(prefix, leaf_tokens)] = leaf_keys_ref[...]
    values[pl.ds(prefix, leaf_tokens)] = leaf_values_ref[...]
    at = lax.broadcasted_iota(jnp.int32, (tokens, node_tokens), 1)
    for n in range(NODES_DEV):
        seen = at < limits_ref[:, n : n + 1]
        mask[:, n * node_tokens : (n + 1) * node_tokens] = jnp.where(seen, 0.0, -1e30)
    at = lax.broadcasted_iota(jnp.int32, (tokens, leaf_tokens), 1)
    seen = (segments_ref[...] == query_segments_ref[...]) & (at <= places_ref[...])
    mask[:, prefix:] = jnp.where(seen, 0.0, -1e30)
    scale = 1.0 / math.sqrt(HEAD_SIZE)
    for h in range(heads_kv * QUERY_PER_KV):
        group = pl.ds(h // QUERY_PER_KV * HEAD_SIZE, HEAD_SIZE)
        head = pl.ds(h * HEAD_SIZE, HEAD_SIZE)
        score = lax.dot_general(
            queries_ref[:, head],
            keys[:, group],
            (((1,), (1,)), ((), ())),
            preferred_element_type=jnp.float32,
        )
        score = score * scale + mask[...]
        top = jnp.max(score, axis=1, keepdims=True)
        expo = jnp.exp(score - top)
        total = jnp.sum(expo, axis=1, keepdims=True)
        summed = jnp.dot(
            expo.astype(jnp.bfloat16), values[:, group], preferred_element_type=jnp.float32
        )
        heads_out[:, head] = (summed / total).astype(jnp.bfloat16)
    fetch.wait()
    span = out_ref.shape[1] // 4
    for n in range(4):
        part = pl.ds(n * span, span)
        out_ref[:, part] = jnp.dot(
            heads_out[...], proj[:, part], preferred_element_type=jnp.float32
        )


def attend(
    queries,
    places,
    query_segments,
    leaf_keys,
    leaf_values,
    fetched,
    segments,
    parents,
    roots,
    lengths,
    out_proj,
):
    is_local, entry, own_pages, sent_pages = fetched
    tokens, leaf_tokens = queries.shape[0], leaf_keys.shape[0]
    middle = jnp.sum(
        (query_segments[:, None] == jnp.arange(REQ_DEV)[None, :]) * parents[None, :], axis=1
    )
    root = jnp.sum((middle[:, None] == jnp.arange(MID_DEV)[None, :]) * roots[None, :], axis=1)
    node = jnp.arange(NODES_DEV)[None, :]
    on_path = (node == root[:, None]) | (node == ROOT_DEV + middle[:, None])
    limits = jnp.where(on_path, lengths[None, :], 0)
    key_count = NODES_DEV * NODE_MAX + leaf_tokens
    scalars = pl.BlockSpec(memory_space=pltpu.SMEM)
    whole = pl.BlockSpec(memory_space=pltpu.VMEM)
    columns = leaf_keys.shape[1]
    heads = queries.shape[1] // HEAD_SIZE
    return pl.pallas_call(
        attend_kernel,
        in_specs=[scalars] * 2 + [whole] * 9 + [pl.BlockSpec(memory_space=pltpu.HBM)],
        out_specs=whole,
        out_shape=jax.ShapeDtypeStruct((tokens, out_proj.shape[1]), jnp.float32),
        scratch_shapes=[
            pltpu.VMEM((key_count, columns), jnp.bfloat16),
            pltpu.VMEM((key_count, columns), jnp.bfloat16),
            pltpu.VMEM((tokens, key_count), jnp.float32),
            pltpu.VMEM(queries.shape, jnp.bfloat16),
            pltpu.VMEM(out_proj.shape, jnp.bfloat16),
            pltpu.SemaphoreType.DMA(()),
        ],
        compiler_params=pltpu.CompilerParams(vmem_limit_bytes=28 * 1024 * 1024),
        cost_estimate=pl.CostEstimate(
            flops=4 * tokens * heads * HEAD_SIZE * key_count + 2 * tokens * out_proj.size,
            bytes_accessed=8 * key_count * columns + 2 * out_proj.size,
            transcendentals=tokens * heads * key_count,
        ),
        name="attend",
    )(
        is_local,
        entry,
        queries,
        limits,
        query_segments[:, None],
        places[:, None],
        segments[None, :],
        own_pages,
        sent_pages,
        leaf_keys,
        leaf_values,
        out_proj,
    )


def fetch_prefix(key_value_pages, page_holder, page_slot):
    groups = lax.axis_size("req")
    myself = lax.axis_index("req")
    holders = page_holder.reshape(groups, -1)
    slots = page_slot.reshape(groups, -1)
    token_count = holders.shape[1]
    room = (token_count // 2 + groups - 2) // (groups - 1)
    earlier = jnp.arange(token_count)[None, :] < jnp.arange(token_count)[:, None]
    same = holders[:, :, None] == holders[:, None, :]
    rank = jnp.sum(same & earlier[None, :, :], axis=-1)
    asked = (holders == myself) & (jnp.arange(groups)[:, None] != myself)
    picked = asked[:, None, :] & (rank[:, None, :] == jnp.arange(room)[None, :, None])
    send_slot = jnp.sum(jnp.where(picked, slots[:, None, :], 0), axis=-1)
    outgoing = jnp.swapaxes(key_value_pages[send_slot.reshape(-1)], 1, 2)
    incoming = lax.all_to_all(outgoing, "req", split_axis=0, concat_axis=0, tiled=True)
    own_holders = lax.dynamic_index_in_dim(holders, myself, 0, keepdims=False)
    own_slots = lax.dynamic_index_in_dim(slots, myself, 0, keepdims=False)
    own_rank = lax.dynamic_index_in_dim(rank, myself, 0, keepdims=False)
    entry = own_holders * room + jnp.minimum(own_rank, room - 1)
    local = jnp.swapaxes(key_value_pages[own_slots], 1, 2)
    return (own_holders == myself).astype(jnp.int32), entry, local, incoming


def gather_tokens(rows):
    inner = lax.axis_size("req") // OUTER
    across = lax.axis_size("mlp") // 2
    column = jnp.concatenate(
        [rows] + [swap(rows, "req", k * inner) for k in range(1, OUTER)], 0
    )
    half = column.shape[0] // 2
    by_x = {k: swap(column, "mlp", 2 * k) for k in range(1, across)}
    by_y = {l: swap(column, "req", l) for l in range(1, inner)}
    blocks = [column] + list(by_x.values()) + list(by_y.values())
    for k in range(1, across):
        for l in range(1, inner):
            blocks.append(swap(by_y[l][:half], "mlp", 2 * k))
            blocks.append(swap(by_x[k][half:], "req", l))
    return jnp.concatenate(blocks, 0)


def scatter_sum(partial, rows):
    inner = lax.axis_size("req") // OUTER
    across = lax.axis_size("mlp") // 2
    size = OUTER * rows
    half = size // 2
    blocks = [partial[i * size : (i + 1) * size] for i in range(across * inner)]
    wide = jnp.float32
    column = blocks[0].astype(wide)
    by_x = {k: blocks[k].astype(wide) for k in range(1, across)}
    by_y = {l: blocks[across - 1 + l].astype(wide) for l in range(1, inner)}
    at = across + inner - 1
    for k in range(1, across):
        for l in range(1, inner):
            first = swap(blocks[at][:half], "mlp", 2 * k).astype(wide)
            second = swap(blocks[at][half:], "req", l).astype(wide)
            by_y[l] = jnp.concatenate([by_y[l][:half] + first, by_y[l][half:]], 0)
            by_x[k] = jnp.concatenate([by_x[k][:half], by_x[k][half:] + second], 0)
            at += 1
    for k in range(1, across):
        column = column + swap(by_x[k].astype(jnp.bfloat16), "mlp", 2 * k).astype(wide)
    for l in range(1, inner):
        column = column + swap(by_y[l].astype(jnp.bfloat16), "req", l).astype(wide)
    total = column[:rows]
    for k in range(1, OUTER):
        part = column[k * rows : (k + 1) * rows].astype(jnp.bfloat16)
        total = total + swap(part, "req", k * inner).astype(wide)
    return total


def sum_cores(projected, rows):
    members = lax.axis_size("mlp")
    wide = jnp.float32
    blocks = [projected[j * rows : (j + 1) * rows] for j in range(members)]
    odd = jnp.concatenate(blocks[1::2], 0).astype(jnp.bfloat16)
    return jnp.concatenate(blocks[0::2], 0) + swap(odd, "mlp", 1).astype(wide)


def sum_across(even, rows):
    members = lax.axis_size("mlp")
    wide = jnp.float32
    total = even[:rows]
    for k in range(1, members // 2):
        part = even[k * rows : (k + 1) * rows].astype(jnp.bfloat16)
        total = total + swap(part, "mlp", 2 * k).astype(wide)
    return total


def gather_heads(rows):
    members = lax.axis_size("mlp")
    place = lax.axis_index("mlp")
    size = rows.shape[0]
    near = [rows] + [swap(rows, "mlp", 2 * k) for k in range(1, members // 2)]
    far = swap(jnp.concatenate(near, 0), "mlp", 1)
    blocks = []
    for k, block in enumerate(near):
        blocks += [block, far[k * size : (k + 1) * size]]
    step = 1
    while step < members:
        flip = (place // step) % 2 == 1
        blocks = [
            jnp.where(flip, blocks[j ^ step], blocks[j]) for j in range(members)
        ]
        step *= 2
    return blocks


def feed_forward_kernel(x_ref, g0, g1, u0, u1, d0, d1, out_ref, wide_rows, down_rows, hidden, sems):
    sources = [g0, u0, g1, u1, d0, d1]
    targets = [wide_rows.at[n] for n in range(4)] + [down_rows.at[n] for n in range(2)]
    copies = [
        pltpu.make_async_copy(source, target, sems.at[n])
        for n, (source, target) in enumerate(zip(sources, targets))
    ]
    for copy in copies:
        copy.start()
    flip = (((1,), (1,)), ((), ()))
    for n in range(2):
        copies[2 * n].wait()
        gate = lax.dot_general(
            x_ref[...], wide_rows[2 * n], flip, preferred_element_type=jnp.float32
        )
        copies[2 * n + 1].wait()
        upper = lax.dot_general(
            x_ref[...], wide_rows[2 * n + 1], flip, preferred_element_type=jnp.float32
        )
        hidden[n] = (gate / (1.0 + jnp.exp(-gate)) * upper).astype(jnp.bfloat16)
    copies[4].wait()
    copies[5].wait()
    span = out_ref.shape[1] // 4
    for n in range(4):
        part = pl.ds(n * span, span)
        total = jnp.dot(hidden[0], down_rows[0, :, part], preferred_element_type=jnp.float32)
        total += jnp.dot(hidden[1], down_rows[1, :, part], preferred_element_type=jnp.float32)
        out_ref[:, part] = total.astype(jnp.bfloat16)


def feed_forward(tokens, gates, uppers, downs):
    rows, width = tokens.shape
    units = gates[0].shape[0]
    far = pl.BlockSpec(memory_space=pltpu.HBM)
    near = pl.BlockSpec(memory_space=pltpu.VMEM)
    return pl.pallas_call(
        feed_forward_kernel,
        in_specs=[near] + [far] * 6,
        out_specs=near,
        out_shape=jax.ShapeDtypeStruct((rows, width), jnp.bfloat16),
        scratch_shapes=[
            pltpu.VMEM((4, units, width), jnp.bfloat16),
            pltpu.VMEM((2, units, width), jnp.bfloat16),
            pltpu.VMEM((2, rows, units), jnp.bfloat16),
            pltpu.SemaphoreType.DMA((6,)),
        ],
        compiler_params=pltpu.CompilerParams(vmem_limit_bytes=40 * 1024 * 1024),
        cost_estimate=pl.CostEstimate(
            flops=12 * rows * width * units,
            bytes_accessed=12 * width * units + 4 * rows * width,
            transcendentals=2 * rows * units,
        ),
        name="feed_forward",
    )(tokens, *gates, *uppers, *downs)


def body(
    queries,
    leaf_keys,
    leaf_token_values,
    key_value_pages,
    page_holder,
    page_slot,
    segment_ids,
    req_parent,
    mid_parent,
    node_len,
    residual,
    out_proj,
    norm_gain,
    gate_proj,
    up_proj,
    down_proj,
    next_gain,
    qkv_proj,
    qkv_bias,
):
    group_tokens = queries.shape[0]
    members = lax.axis_size("mlp")
    place = lax.axis_index("mlp")
    owned = group_tokens // members
    rows = owned // CHUNKS
    gate_rows, up_rows = gate_proj.T, up_proj.T
    gates = [gate_rows, swap(gate_rows, "mlp", 1)]
    uppers = [up_rows, swap(up_rows, "mlp", 1)]
    downs = [down_proj, swap(down_proj, "mlp", 1)]
    fetched = fetch_prefix(key_value_pages, page_holder, page_slot)
    starts = [
        (place ^ j) * owned + chunk * rows for chunk in range(CHUNKS) for j in range(members)
    ]

    def picked(array):
        return jnp.concatenate([lax.dynamic_slice_in_dim(array, s, rows, 0) for s in starts], 0)

    places = jnp.concatenate([s + jnp.arange(rows) for s in starts], 0)
    asked, fetched, gates, uppers, downs = lax.optimization_barrier(
        (picked(queries), fetched, gates, uppers, downs)
    )
    projected = attend(
        asked,
        places,
        picked(segment_ids),
        leaf_keys,
        leaf_token_values,
        fetched,
        segment_ids,
        req_parent[0],
        mid_parent[0],
        node_len[0],
        out_proj,
    )
    span = members * rows
    evens = [sum_cores(projected[c * span : (c + 1) * span], rows) for c in range(CHUNKS)]
    streams, mixed = [], []
    for chunk in range(CHUNKS):
        own = lax.dynamic_slice_in_dim(residual, place * owned + chunk * rows, rows, 0)
        summed = sum_across(evens[chunk], rows)
        streams.append((own.astype(jnp.float32) + summed).astype(jnp.bfloat16))
    for chunk in range(CHUNKS):
        tokens = gather_tokens(rms_norm(streams[chunk], norm_gain))
        mixed.append(feed_forward(tokens, gates, uppers, downs))
    layer_rows, next_rows = [], []
    for chunk in range(CHUNKS):
        summed = scatter_sum(mixed[chunk], rows)
        layer = (streams[chunk].astype(jnp.float32) + summed).astype(jnp.bfloat16)
        layer_rows.append(layer)
        next_rows.append(gather_heads(rms_norm(layer, next_gain)))
    layer_out = jnp.concatenate(layer_rows, 0)
    next_normed = jnp.concatenate(
        [next_rows[c][j] for j in range(members) for c in range(CHUNKS)], 0
    )
    qkv_out = (
        jnp.dot(next_normed, qkv_proj, preferred_element_type=jnp.float32) + qkv_bias
    ).astype(jnp.bfloat16)
    return (layer_out, qkv_out)


def solution(mesh):
    placed = (
        P("req", "mlp"),
        P("req", "mlp"),
        P("req", "mlp"),
        P("req", None, None, "mlp"),
        P(),
        P(),
        P("req"),
        P("req", None),
        P("req", None),
        P("req", None),
        P("req", None),
        P("mlp", None),
        P(),
        P(None, ("req", "mlp")),
        P(None, ("req", "mlp")),
        P(("req", "mlp"), None),
        P(),
        P(None, "mlp"),
        P("mlp"),
    )
    return jax.shard_map(
        body,
        mesh=mesh,
        in_specs=placed,
        out_specs=(P(("req", "mlp"), None), P("req", "mlp")),
        check_vma=False,
    )
```

```python
import math

import jax
import jax.numpy as jnp
from jax import lax
from jax.experimental import pallas as pl
from jax.experimental.pallas import tpu as pltpu
from jax.sharding import PartitionSpec as P

HEAD_SIZE = 128
QUERY_PER_KV = 5
REQ_DEV = 8
ROOT_DEV = 2
MID_DEV = 4
NODES_DEV = 6
NODE_MAX = 256
OUTER = 4
CHUNKS = 2


EPS = 1e-06


def rms_norm(stream, gain):
    values = stream.astype(jnp.float32)
    mean_sq = jnp.mean(values * values, axis=-1, keepdims=True)
    return (values * lax.rsqrt(mean_sq + EPS) * gain).astype(jnp.bfloat16)


def swap(array, axis, step):
    return lax.ppermute(array, axis, [(i, i ^ step) for i in range(lax.axis_size(axis))])


def attend_kernel(
    local_ref,
    entry_ref,
    queries_ref,
    limits_ref,
    query_segments_ref,
    places_ref,
    segments_ref,
    own_pages_ref,
    sent_pages_ref,
    leaf_keys_ref,
    leaf_values_ref,
    proj_ref,
    out_ref,
    keys,
    values,
    mask,
    heads_out,
    proj,
    proj_sem,
):
    fetch = pltpu.make_async_copy(proj_ref, proj, proj_sem)
    fetch.start()
    tokens = queries_ref.shape[0]
    page = own_pages_ref.shape[2]
    pages = own_pages_ref.shape[0]
    prefix = pages * page
    node_tokens = prefix // NODES_DEV
    leaf_tokens = leaf_keys_ref.shape[0]
    heads_kv = leaf_keys_ref.shape[1] // HEAD_SIZE
    for p in range(pages):
        span = pl.ds(p * page, page)

        @pl.when(local_ref[p] == 1)
        def _():
            keys[span] = own_pages_ref[p, 0]
            values[span] = own_pages_ref[p, 1]

        @pl.when(local_ref[p] == 0)
        def _():
            keys[span] = sent_pages_ref[entry_ref[p], 0]
            values[span] = sent_pages_ref[entry_ref[p], 1]

    keys[pl.ds(prefix, leaf_tokens)] = leaf_keys_ref[...]
    values[pl.ds(prefix, leaf_tokens)] = leaf_values_ref[...]
    at = lax.broadcasted_iota(jnp.int32, (tokens, node_tokens), 1)
    for n in range(NODES_DEV):
        seen = at < limits_ref[:, n : n + 1]
        mask[:, n * node_tokens : (n + 1) * node_tokens] = jnp.where(seen, 0.0, -1e30)
    at = lax.broadcasted_iota(jnp.int32, (tokens, leaf_tokens), 1)
    seen = (segments_ref[...] == query_segments_ref[...]) & (at <= places_ref[...])
    mask[:, prefix:] = jnp.where(seen, 0.0, -1e30)
    scale = 1.0 / math.sqrt(HEAD_SIZE)
    for h in range(heads_kv * QUERY_PER_KV):
        group = pl.ds(h // QUERY_PER_KV * HEAD_SIZE, HEAD_SIZE)
        head = pl.ds(h * HEAD_SIZE, HEAD_SIZE)
        score = lax.dot_general(
            queries_ref[:, head],
            keys[:, group],
            (((1,), (1,)), ((), ())),
            preferred_element_type=jnp.float32,
        )
        score = score * scale + mask[...]
        top = jnp.max(score, axis=1, keepdims=True)
        expo = jnp.exp(score - top)
        total = jnp.sum(expo, axis=1, keepdims=True)
        summed = jnp.dot(
            expo.astype(jnp.bfloat16), values[:, group], preferred_element_type=jnp.float32
        )
        heads_out[:, head] = (summed / total).astype(jnp.bfloat16)
    fetch.wait()
    span = out_ref.shape[1] // 4
    for n in range(4):
        part = pl.ds(n * span, span)
        out_ref[:, part] = jnp.dot(
            heads_out[...], proj[:, part], preferred_element_type=jnp.float32
        )


def attend(
    queries,
    places,
    query_segments,
    leaf_keys,
    leaf_values,
    fetched,
    segments,
    parents,
    roots,
    lengths,
    out_proj,
):
    is_local, entry, own_pages, sent_pages = fetched
    tokens, leaf_tokens = queries.shape[0], leaf_keys.shape[0]
    middle = jnp.sum(
        (query_segments[:, None] == jnp.arange(REQ_DEV)[None, :]) * parents[None, :], axis=1
    )
    root = jnp.sum((middle[:, None] == jnp.arange(MID_DEV)[None, :]) * roots[None, :], axis=1)
    node = jnp.arange(NODES_DEV)[None, :]
    on_path = (node == root[:, None]) | (node == ROOT_DEV + middle[:, None])
    limits = jnp.where(on_path, lengths[None, :], 0)
    key_count = NODES_DEV * NODE_MAX + leaf_tokens
    scalars = pl.BlockSpec(memory_space=pltpu.SMEM)
    whole = pl.BlockSpec(memory_space=pltpu.VMEM)
    columns = leaf_keys.shape[1]
    heads = queries.shape[1] // HEAD_SIZE
    return pl.pallas_call(
        attend_kernel,
        in_specs=[scalars] * 2 + [whole] * 9 + [pl.BlockSpec(memory_space=pltpu.HBM)],
        out_specs=whole,
        out_shape=jax.ShapeDtypeStruct((tokens, out_proj.shape[1]), jnp.float32),
        scratch_shapes=[
            pltpu.VMEM((key_count, columns), jnp.bfloat16),
            pltpu.VMEM((key_count, columns), jnp.bfloat16),
            pltpu.VMEM((tokens, key_count), jnp.float32),
            pltpu.VMEM(queries.shape, jnp.bfloat16),
            pltpu.VMEM(out_proj.shape, jnp.bfloat16),
            pltpu.SemaphoreType.DMA(()),
        ],
        compiler_params=pltpu.CompilerParams(vmem_limit_bytes=51 * 1024 * 1024),
        cost_estimate=pl.CostEstimate(
            flops=4 * tokens * heads * HEAD_SIZE * key_count + 2 * tokens * out_proj.size,
            bytes_accessed=8 * key_count * columns + 2 * out_proj.size,
            transcendentals=tokens * heads * key_count,
        ),
        name="attend",
    )(
        is_local,
        entry,
        queries,
        limits,
        query_segments[:, None],
        places[:, None],
        segments[None, :],
        own_pages,
        sent_pages,
        leaf_keys,
        leaf_values,
        out_proj,
    )


def fetch_prefix(key_value_pages, page_holder, page_slot):
    groups = lax.axis_size("req")
    myself = lax.axis_index("req")
    holders = page_holder.reshape(groups, -1)
    slots = page_slot.reshape(groups, -1)
    token_count = holders.shape[1]
    room = (token_count // 2 + groups - 2) // (groups - 1)
    earlier = jnp.arange(token_count)[None, :] < jnp.arange(token_count)[:, None]
    same = holders[:, :, None] == holders[:, None, :]
    rank = jnp.sum(same & earlier[None, :, :], axis=-1)
    asked = (holders == myself) & (jnp.arange(groups)[:, None] != myself)
    picked = asked[:, None, :] & (rank[:, None, :] == jnp.arange(room)[None, :, None])
    send_slot = jnp.sum(jnp.where(picked, slots[:, None, :], 0), axis=-1)
    outgoing = jnp.swapaxes(key_value_pages[send_slot.reshape(-1)], 1, 2)
    incoming = lax.all_to_all(outgoing, "req", split_axis=0, concat_axis=0, tiled=True)
    own_holders = lax.dynamic_index_in_dim(holders, myself, 0, keepdims=False)
    own_slots = lax.dynamic_index_in_dim(slots, myself, 0, keepdims=False)
    own_rank = lax.dynamic_index_in_dim(rank, myself, 0, keepdims=False)
    entry = own_holders * room + jnp.minimum(own_rank, room - 1)
    local = jnp.swapaxes(key_value_pages[own_slots], 1, 2)
    return (own_holders == myself).astype(jnp.int32), entry, local, incoming


def gather_tokens(rows):
    inner = lax.axis_size("req") // OUTER
    across = lax.axis_size("mlp") // 2
    column = jnp.concatenate(
        [rows] + [swap(rows, "req", k * inner) for k in range(1, OUTER)], 0
    )
    half = column.shape[0] // 2
    by_x = {k: swap(column, "mlp", 2 * k) for k in range(1, across)}
    by_y = {l: swap(column, "req", l) for l in range(1, inner)}
    blocks = [column] + list(by_x.values()) + list(by_y.values())
    for k in range(1, across):
        for l in range(1, inner):
            blocks.append(swap(by_y[l][:half], "mlp", 2 * k))
            blocks.append(swap(by_x[k][half:], "req", l))
    return jnp.concatenate(blocks, 0)


def scatter_sum(partial, rows):
    inner = lax.axis_size("req") // OUTER
    across = lax.axis_size("mlp") // 2
    size = OUTER * rows
    half = size // 2
    blocks = [partial[i * size : (i + 1) * size] for i in range(across * inner)]
    wide = jnp.float32
    column = blocks[0].astype(wide)
    by_x = {k: blocks[k].astype(wide) for k in range(1, across)}
    by_y = {l: blocks[across - 1 + l].astype(wide) for l in range(1, inner)}
    at = across + inner - 1
    for k in range(1, across):
        for l in range(1, inner):
            first = swap(blocks[at][:half], "mlp", 2 * k).astype(wide)
            second = swap(blocks[at][half:], "req", l).astype(wide)
            by_y[l] = jnp.concatenate([by_y[l][:half] + first, by_y[l][half:]], 0)
            by_x[k] = jnp.concatenate([by_x[k][:half], by_x[k][half:] + second], 0)
            at += 1
    by_x = {k: part.astype(jnp.bfloat16) for k, part in by_x.items()}
    by_y = {l: part.astype(jnp.bfloat16) for l, part in by_y.items()}
    for k in range(1, across):
        column = column + swap(by_x[k], "mlp", 2 * k).astype(wide)
    for l in range(1, inner):
        column = column + swap(by_y[l], "req", l).astype(wide)
    total = column[:rows]
    for k in range(1, OUTER):
        part = column[k * rows : (k + 1) * rows].astype(jnp.bfloat16)
        total = total + swap(part, "req", k * inner).astype(wide)
    return total, (by_x, by_y)


def sum_cores(projected, rows):
    members = lax.axis_size("mlp")
    wide = jnp.float32
    blocks = [projected[j * rows : (j + 1) * rows] for j in range(members)]
    odd = jnp.concatenate(blocks[1::2], 0).astype(jnp.bfloat16)
    return jnp.concatenate(blocks[0::2], 0) + swap(odd, "mlp", 1).astype(wide)


def sum_across(even, rows):
    members = lax.axis_size("mlp")
    wide = jnp.float32
    total = even[:rows]
    for k in range(1, members // 2):
        part = even[k * rows : (k + 1) * rows].astype(jnp.bfloat16)
        total = total + swap(part, "mlp", 2 * k).astype(wide)
    return total


def gather_heads(rows):
    members = lax.axis_size("mlp")
    place = lax.axis_index("mlp")
    size = rows.shape[0]
    near = [rows] + [swap(rows, "mlp", 2 * k) for k in range(1, members // 2)]
    far = swap(jnp.concatenate(near, 0), "mlp", 1)
    blocks = []
    for k, block in enumerate(near):
        blocks += [block, far[k * size : (k + 1) * size]]
    step = 1
    while step < members:
        flip = (place // step) % 2 == 1
        blocks = [
            jnp.where(flip, blocks[j ^ step], blocks[j]) for j in range(members)
        ]
        step *= 2
    return blocks


def feed_forward_kernel(x_ref, g0, g1, u0, u1, d0, d1, out_ref, wide_rows, down_rows, hidden, sems):
    sources = [g0, u0, g1, u1, d0, d1]
    targets = [wide_rows.at[n] for n in range(4)] + [down_rows.at[n] for n in range(2)]
    copies = [
        pltpu.make_async_copy(source, target, sems.at[n])
        for n, (source, target) in enumerate(zip(sources, targets))
    ]
    for copy in copies:
        copy.start()
    flip = (((1,), (1,)), ((), ()))
    for n in range(2):
        copies[2 * n].wait()
        gate = lax.dot_general(
            x_ref[...], wide_rows[2 * n], flip, preferred_element_type=jnp.float32
        )
        copies[2 * n + 1].wait()
        upper = lax.dot_general(
            x_ref[...], wide_rows[2 * n + 1], flip, preferred_element_type=jnp.float32
        )
        hidden[n] = (gate / (1.0 + jnp.exp(-gate)) * upper).astype(jnp.bfloat16)
    copies[4].wait()
    copies[5].wait()
    span = out_ref.shape[1] // 4
    for n in range(4):
        part = pl.ds(n * span, span)
        total = jnp.dot(hidden[0], down_rows[0, :, part], preferred_element_type=jnp.float32)
        total += jnp.dot(hidden[1], down_rows[1, :, part], preferred_element_type=jnp.float32)
        out_ref[:, part] = total.astype(jnp.bfloat16)


def feed_forward(tokens, gates, uppers, downs):
    rows, width = tokens.shape
    units = gates[0].shape[0]
    far = pl.BlockSpec(memory_space=pltpu.HBM)
    near = pl.BlockSpec(memory_space=pltpu.VMEM)
    return pl.pallas_call(
        feed_forward_kernel,
        in_specs=[near] + [far] * 6,
        out_specs=near,
        out_shape=jax.ShapeDtypeStruct((rows, width), jnp.bfloat16),
        scratch_shapes=[
            pltpu.VMEM((4, units, width), jnp.bfloat16),
            pltpu.VMEM((2, units, width), jnp.bfloat16),
            pltpu.VMEM((2, rows, units), jnp.bfloat16),
            pltpu.SemaphoreType.DMA((6,)),
        ],
        compiler_params=pltpu.CompilerParams(vmem_limit_bytes=40 * 1024 * 1024),
        cost_estimate=pl.CostEstimate(
            flops=12 * rows * width * units,
            bytes_accessed=12 * width * units + 4 * rows * width,
            transcendentals=2 * rows * units,
        ),
        name="feed_forward",
    )(tokens, *gates, *uppers, *downs)


def hold_kernel(source_ref, out_ref, sem):
    copy = pltpu.make_async_copy(source_ref, out_ref, sem)
    copy.start()
    copy.wait()


def hold(array):
    return pl.pallas_call(
        hold_kernel,
        in_specs=[pl.BlockSpec(memory_space=pltpu.HBM)],
        out_specs=pl.BlockSpec(memory_space=pltpu.VMEM),
        out_shape=pltpu.VMEM(array.shape, array.dtype),
        scratch_shapes=[pltpu.SemaphoreType.DMA(())],
        compiler_params=pltpu.CompilerParams(vmem_limit_bytes=2 * 1024 * 1024),
        cost_estimate=pl.CostEstimate(
            flops=0, bytes_accessed=4 * array.size, transcendentals=0
        ),
        name="hold",
    )(array)


def body(
    queries,
    leaf_keys,
    leaf_token_values,
    key_value_pages,
    page_holder,
    page_slot,
    segment_ids,
    req_parent,
    mid_parent,
    node_len,
    residual,
    out_proj,
    norm_gain,
    gate_proj,
    up_proj,
    down_proj,
    next_gain,
    qkv_proj,
    qkv_bias,
):
    group_tokens = queries.shape[0]
    members = lax.axis_size("mlp")
    place = lax.axis_index("mlp")
    owned = group_tokens // members
    rows = owned // CHUNKS
    gate_rows, up_rows = gate_proj.T, up_proj.T
    gates = [gate_rows, swap(gate_rows, "mlp", 1)]
    uppers = [up_rows, swap(up_rows, "mlp", 1)]
    downs = [down_proj, swap(down_proj, "mlp", 1)]
    fetched = fetch_prefix(key_value_pages, page_holder, page_slot)
    starts = [
        (place ^ j) * owned + chunk * rows for chunk in range(CHUNKS) for j in range(members)
    ]

    def picked(array):
        return jnp.concatenate([lax.dynamic_slice_in_dim(array, s, rows, 0) for s in starts], 0)

    places = jnp.concatenate([s + jnp.arange(rows) for s in starts], 0)
    asked, fetched, gates, uppers, downs = lax.optimization_barrier(
        (picked(queries), fetched, gates, uppers, downs)
    )
    projected = attend(
        asked,
        places,
        picked(segment_ids),
        leaf_keys,
        leaf_token_values,
        fetched,
        segment_ids,
        req_parent[0],
        mid_parent[0],
        node_len[0],
        out_proj,
    )
    span = members * rows
    evens = [sum_cores(projected[c * span : (c + 1) * span], rows) for c in range(CHUNKS)]
    streams, mixed = [], []
    for chunk in range(CHUNKS):
        own = lax.dynamic_slice_in_dim(residual, place * owned + chunk * rows, rows, 0)
        summed = sum_across(evens[chunk], rows)
        streams.append((own.astype(jnp.float32) + summed).astype(jnp.bfloat16))
    for chunk in range(CHUNKS):
        tokens = gather_tokens(rms_norm(streams[chunk], norm_gain))
        mixed.append(feed_forward(tokens, gates, uppers, downs))
    layer_rows, next_rows, sent = [], [], []
    for chunk in range(CHUNKS):
        summed, sides = scatter_sum(mixed[chunk], rows)
        sent.append(sides)
        layer = (streams[chunk].astype(jnp.float32) + summed).astype(jnp.bfloat16)
        layer_rows.append(layer)
        next_rows.append(gather_heads(rms_norm(layer, next_gain)))
    layer_out = jnp.concatenate(layer_rows, 0)
    held = hold(lax.optimization_barrier((qkv_proj, sent))[0])
    next_normed = jnp.concatenate(
        [next_rows[c][j] for j in range(members) for c in range(CHUNKS)], 0
    )
    qkv_out = (
        jnp.dot(next_normed, held, preferred_element_type=jnp.float32) + qkv_bias
    ).astype(jnp.bfloat16)
    return (layer_out, qkv_out)


def solution(mesh):
    placed = (
        P("req", "mlp"),
        P("req", "mlp"),
        P("req", "mlp"),
        P("req", None, None, "mlp"),
        P(),
        P(),
        P("req"),
        P("req", None),
        P("req", None),
        P("req", None),
        P("req", None),
        P("mlp", None),
        P(),
        P(None, ("req", "mlp")),
        P(None, ("req", "mlp")),
        P(("req", "mlp"), None),
        P(),
        P(None, "mlp"),
        P("mlp"),
    )
    return jax.shard_map(
        body,
        mesh=mesh,
        in_specs=placed,
        out_specs=(P(("req", "mlp"), None), P("req", "mlp")),
        check_vma=False,
    )
```

```python
import math

import jax
import jax.numpy as jnp
from jax import lax
from jax.experimental import pallas as pl
from jax.experimental.pallas import tpu as pltpu
from jax.sharding import PartitionSpec as P

HEAD_SIZE = 128
QUERY_PER_KV = 5
REQ_DEV = 8
ROOT_DEV = 2
MID_DEV = 4
NODES_DEV = 6
NODE_MAX = 256
OUTER = 4
CHUNKS = 2


EPS = 1e-06


def rms_norm(stream, gain):
    values = stream.astype(jnp.float32)
    mean_sq = jnp.mean(values * values, axis=-1, keepdims=True)
    return (values * lax.rsqrt(mean_sq + EPS) * gain).astype(jnp.bfloat16)


def swap(array, axis, step):
    return lax.ppermute(array, axis, [(i, i ^ step) for i in range(lax.axis_size(axis))])


def attend_kernel(
    local_ref,
    entry_ref,
    queries_ref,
    limits_ref,
    query_segments_ref,
    places_ref,
    segments_ref,
    own_pages_ref,
    sent_pages_ref,
    leaf_keys_ref,
    leaf_values_ref,
    proj_ref,
    kept_ref,
    sent_ref,
    keys,
    values,
    mask,
    heads_out,
    proj,
    proj_sem,
):
    fetch = pltpu.make_async_copy(proj_ref, proj, proj_sem)
    fetch.start()
    tokens = queries_ref.shape[0]
    page = own_pages_ref.shape[2]
    pages = own_pages_ref.shape[0]
    prefix = pages * page
    node_tokens = prefix // NODES_DEV
    leaf_tokens = leaf_keys_ref.shape[0]
    heads_kv = leaf_keys_ref.shape[1] // HEAD_SIZE
    for p in range(pages):
        span = pl.ds(p * page, page)

        @pl.when(local_ref[p] == 1)
        def _():
            keys[span] = own_pages_ref[p, 0]
            values[span] = own_pages_ref[p, 1]

        @pl.when(local_ref[p] == 0)
        def _():
            keys[span] = sent_pages_ref[entry_ref[p], 0]
            values[span] = sent_pages_ref[entry_ref[p], 1]

    keys[pl.ds(prefix, leaf_tokens)] = leaf_keys_ref[...]
    values[pl.ds(prefix, leaf_tokens)] = leaf_values_ref[...]
    at = lax.broadcasted_iota(jnp.int32, (tokens, node_tokens), 1)
    for n in range(NODES_DEV):
        seen = at < limits_ref[:, n : n + 1]
        mask[:, n * node_tokens : (n + 1) * node_tokens] = jnp.where(seen, 0.0, -1e30)
    at = lax.broadcasted_iota(jnp.int32, (tokens, leaf_tokens), 1)
    seen = (segments_ref[...] == query_segments_ref[...]) & (at <= places_ref[...])
    mask[:, prefix:] = jnp.where(seen, 0.0, -1e30)
    scale = 1.0 / math.sqrt(HEAD_SIZE)
    for h in range(heads_kv * QUERY_PER_KV):
        group = pl.ds(h // QUERY_PER_KV * HEAD_SIZE, HEAD_SIZE)
        head = pl.ds(h * HEAD_SIZE, HEAD_SIZE)
        score = lax.dot_general(
            queries_ref[:, head],
            keys[:, group],
            (((1,), (1,)), ((), ())),
            preferred_element_type=jnp.float32,
        )
        score = score * scale + mask[...]
        top = jnp.max(score, axis=1, keepdims=True)
        expo = jnp.exp(score - top)
        total = jnp.sum(expo, axis=1, keepdims=True)
        summed = jnp.dot(
            expo.astype(jnp.bfloat16), values[:, group], preferred_element_type=jnp.float32
        )
        heads_out[:, head] = (summed / total).astype(jnp.bfloat16)
    fetch.wait()
    half = tokens // 2
    span = kept_ref.shape[1] // 4
    for n in range(4):
        part = pl.ds(n * span, span)
        product = jnp.dot(heads_out[...], proj[:, part], preferred_element_type=jnp.float32)
        kept_ref[:, part] = product[:half]
        sent_ref[:, part] = product[half:].astype(jnp.bfloat16)


def attend(
    queries,
    places,
    query_segments,
    leaf_keys,
    leaf_values,
    fetched,
    segments,
    parents,
    roots,
    lengths,
    out_proj,
):
    is_local, entry, own_pages, sent_pages = fetched
    tokens, leaf_tokens = queries.shape[0], leaf_keys.shape[0]
    middle = jnp.sum(
        (query_segments[:, None] == jnp.arange(REQ_DEV)[None, :]) * parents[None, :], axis=1
    )
    root = jnp.sum((middle[:, None] == jnp.arange(MID_DEV)[None, :]) * roots[None, :], axis=1)
    node = jnp.arange(NODES_DEV)[None, :]
    on_path = (node == root[:, None]) | (node == ROOT_DEV + middle[:, None])
    limits = jnp.where(on_path, lengths[None, :], 0)
    key_count = NODES_DEV * NODE_MAX + leaf_tokens
    scalars = pl.BlockSpec(memory_space=pltpu.SMEM)
    whole = pl.BlockSpec(memory_space=pltpu.VMEM)
    columns = leaf_keys.shape[1]
    heads = queries.shape[1] // HEAD_SIZE
    return pl.pallas_call(
        attend_kernel,
        in_specs=[scalars] * 2 + [whole] * 9 + [pl.BlockSpec(memory_space=pltpu.HBM)],
        out_specs=[whole, whole],
        out_shape=[
            jax.ShapeDtypeStruct((tokens // 2, out_proj.shape[1]), jnp.float32),
            jax.ShapeDtypeStruct((tokens // 2, out_proj.shape[1]), jnp.bfloat16),
        ],
        scratch_shapes=[
            pltpu.VMEM((key_count, columns), jnp.bfloat16),
            pltpu.VMEM((key_count, columns), jnp.bfloat16),
            pltpu.VMEM((tokens, key_count), jnp.float32),
            pltpu.VMEM(queries.shape, jnp.bfloat16),
            pltpu.VMEM(out_proj.shape, jnp.bfloat16),
            pltpu.SemaphoreType.DMA(()),
        ],
        compiler_params=pltpu.CompilerParams(vmem_limit_bytes=51 * 1024 * 1024),
        cost_estimate=pl.CostEstimate(
            flops=4 * tokens * heads * HEAD_SIZE * key_count + 2 * tokens * out_proj.size,
            bytes_accessed=8 * key_count * columns + 2 * out_proj.size,
            transcendentals=tokens * heads * key_count,
        ),
        name="attend",
    )(
        is_local,
        entry,
        queries,
        limits,
        query_segments[:, None],
        places[:, None],
        segments[None, :],
        own_pages,
        sent_pages,
        leaf_keys,
        leaf_values,
        out_proj,
    )


def fetch_prefix(key_value_pages, page_holder, page_slot):
    groups = lax.axis_size("req")
    myself = lax.axis_index("req")
    holders = page_holder.reshape(groups, -1)
    slots = page_slot.reshape(groups, -1)
    token_count = holders.shape[1]
    room = (token_count // 2 + groups - 2) // (groups - 1)
    earlier = jnp.arange(token_count)[None, :] < jnp.arange(token_count)[:, None]
    same = holders[:, :, None] == holders[:, None, :]
    rank = jnp.sum(same & earlier[None, :, :], axis=-1)
    asked = (holders == myself) & (jnp.arange(groups)[:, None] != myself)
    picked = asked[:, None, :] & (rank[:, None, :] == jnp.arange(room)[None, :, None])
    send_slot = jnp.sum(jnp.where(picked, slots[:, None, :], 0), axis=-1)
    outgoing = jnp.swapaxes(key_value_pages[send_slot.reshape(-1)], 1, 2)
    incoming = lax.all_to_all(outgoing, "req", split_axis=0, concat_axis=0, tiled=True)
    own_holders = lax.dynamic_index_in_dim(holders, myself, 0, keepdims=False)
    own_slots = lax.dynamic_index_in_dim(slots, myself, 0, keepdims=False)
    own_rank = lax.dynamic_index_in_dim(rank, myself, 0, keepdims=False)
    entry = own_holders * room + jnp.minimum(own_rank, room - 1)
    local = jnp.swapaxes(key_value_pages[own_slots], 1, 2)
    return (own_holders == myself).astype(jnp.int32), entry, local, incoming


def gather_tokens(rows):
    inner = lax.axis_size("req") // OUTER
    across = lax.axis_size("mlp") // 2
    column = jnp.concatenate(
        [rows] + [swap(rows, "req", k * inner) for k in range(1, OUTER)], 0
    )
    half = column.shape[0] // 2
    by_x = {k: swap(column, "mlp", 2 * k) for k in range(1, across)}
    by_y = {l: swap(column, "req", l) for l in range(1, inner)}
    blocks = [column] + list(by_x.values()) + list(by_y.values())
    for k in range(1, across):
        for l in range(1, inner):
            blocks.append(swap(by_y[l][:half], "mlp", 2 * k))
            blocks.append(swap(by_x[k][half:], "req", l))
    return jnp.concatenate(blocks, 0)


def scatter_sum(partial, rows):
    inner = lax.axis_size("req") // OUTER
    across = lax.axis_size("mlp") // 2
    size = OUTER * rows
    half = size // 2
    blocks = [partial[i * size : (i + 1) * size] for i in range(across * inner)]
    wide = jnp.float32
    column = blocks[0].astype(wide)
    by_x = {k: blocks[k].astype(wide) for k in range(1, across)}
    by_y = {l: blocks[across - 1 + l].astype(wide) for l in range(1, inner)}
    at = across + inner - 1
    for k in range(1, across):
        for l in range(1, inner):
            first = swap(blocks[at][:half], "mlp", 2 * k).astype(wide)
            second = swap(blocks[at][half:], "req", l).astype(wide)
            by_y[l] = jnp.concatenate([by_y[l][:half] + first, by_y[l][half:]], 0)
            by_x[k] = jnp.concatenate([by_x[k][:half], by_x[k][half:] + second], 0)
            at += 1
    by_x = {k: part.astype(jnp.bfloat16) for k, part in by_x.items()}
    by_y = {l: part.astype(jnp.bfloat16) for l, part in by_y.items()}
    for k in range(1, across):
        column = column + swap(by_x[k], "mlp", 2 * k).astype(wide)
    for l in range(1, inner):
        column = column + swap(by_y[l], "req", l).astype(wide)
    total = column[:rows]
    for k in range(1, OUTER):
        part = column[k * rows : (k + 1) * rows].astype(jnp.bfloat16)
        total = total + swap(part, "req", k * inner).astype(wide)
    return total, (by_x, by_y)


def sum_heads(kept, sent, rows):
    wide = jnp.float32
    even = kept + swap(sent, "mlp", 1).astype(wide)
    total = even[:rows]
    for k in range(1, kept.shape[0] // rows):
        part = even[k * rows : (k + 1) * rows].astype(jnp.bfloat16)
        total = total + swap(part, "mlp", 2 * k).astype(wide)
    return total


def gather_heads(rows):
    members = lax.axis_size("mlp")
    place = lax.axis_index("mlp")
    size = rows.shape[0]
    near = [rows] + [swap(rows, "mlp", 2 * k) for k in range(1, members // 2)]
    far = swap(jnp.concatenate(near, 0), "mlp", 1)
    blocks = []
    for k, block in enumerate(near):
        blocks += [block, far[k * size : (k + 1) * size]]
    step = 1
    while step < members:
        flip = (place // step) % 2 == 1
        blocks = [
            jnp.where(flip, blocks[j ^ step], blocks[j]) for j in range(members)
        ]
        step *= 2
    return blocks


def feed_forward_kernel(x_ref, g0, g1, u0, u1, d0, d1, out_ref, wide_rows, down_rows, hidden, sems):
    sources = [g0, u0, g1, u1, d0, d1]
    targets = [wide_rows.at[n] for n in range(4)] + [down_rows.at[n] for n in range(2)]
    copies = [
        pltpu.make_async_copy(source, target, sems.at[n])
        for n, (source, target) in enumerate(zip(sources, targets))
    ]
    for copy in copies:
        copy.start()
    flip = (((1,), (1,)), ((), ()))
    for n in range(2):
        copies[2 * n].wait()
        gate = lax.dot_general(
            x_ref[...], wide_rows[2 * n], flip, preferred_element_type=jnp.float32
        )
        copies[2 * n + 1].wait()
        upper = lax.dot_general(
            x_ref[...], wide_rows[2 * n + 1], flip, preferred_element_type=jnp.float32
        )
        hidden[n] = (gate / (1.0 + jnp.exp(-gate)) * upper).astype(jnp.bfloat16)
    copies[4].wait()
    copies[5].wait()
    span = out_ref.shape[1] // 4
    for n in range(4):
        part = pl.ds(n * span, span)
        total = jnp.dot(hidden[0], down_rows[0, :, part], preferred_element_type=jnp.float32)
        total += jnp.dot(hidden[1], down_rows[1, :, part], preferred_element_type=jnp.float32)
        out_ref[:, part] = total.astype(jnp.bfloat16)


def feed_forward(tokens, gates, uppers, downs):
    rows, width = tokens.shape
    units = gates[0].shape[0]
    far = pl.BlockSpec(memory_space=pltpu.HBM)
    near = pl.BlockSpec(memory_space=pltpu.VMEM)
    return pl.pallas_call(
        feed_forward_kernel,
        in_specs=[near] + [far] * 6,
        out_specs=near,
        out_shape=jax.ShapeDtypeStruct((rows, width), jnp.bfloat16),
        scratch_shapes=[
            pltpu.VMEM((4, units, width), jnp.bfloat16),
            pltpu.VMEM((2, units, width), jnp.bfloat16),
            pltpu.VMEM((2, rows, units), jnp.bfloat16),
            pltpu.SemaphoreType.DMA((6,)),
        ],
        compiler_params=pltpu.CompilerParams(vmem_limit_bytes=40 * 1024 * 1024),
        cost_estimate=pl.CostEstimate(
            flops=12 * rows * width * units,
            bytes_accessed=12 * width * units + 4 * rows * width,
            transcendentals=2 * rows * units,
        ),
        name="feed_forward",
    )(tokens, *gates, *uppers, *downs)


def hold_kernel(source_ref, out_ref, sem):
    copy = pltpu.make_async_copy(source_ref, out_ref, sem)
    copy.start()
    copy.wait()


def hold(array):
    return pl.pallas_call(
        hold_kernel,
        in_specs=[pl.BlockSpec(memory_space=pltpu.HBM)],
        out_specs=pl.BlockSpec(memory_space=pltpu.VMEM),
        out_shape=pltpu.VMEM(array.shape, array.dtype),
        scratch_shapes=[pltpu.SemaphoreType.DMA(())],
        compiler_params=pltpu.CompilerParams(vmem_limit_bytes=2 * 1024 * 1024),
        cost_estimate=pl.CostEstimate(
            flops=0, bytes_accessed=4 * array.size, transcendentals=0
        ),
        name="hold",
    )(array)


def body(
    queries,
    leaf_keys,
    leaf_token_values,
    key_value_pages,
    page_holder,
    page_slot,
    segment_ids,
    req_parent,
    mid_parent,
    node_len,
    residual,
    out_proj,
    norm_gain,
    gate_proj,
    up_proj,
    down_proj,
    next_gain,
    qkv_proj,
    qkv_bias,
):
    group_tokens = queries.shape[0]
    members = lax.axis_size("mlp")
    place = lax.axis_index("mlp")
    owned = group_tokens // members
    rows = owned // CHUNKS
    gate_rows, up_rows = gate_proj.T, up_proj.T
    gates = [gate_rows, swap(gate_rows, "mlp", 1)]
    uppers = [up_rows, swap(up_rows, "mlp", 1)]
    downs = [down_proj, swap(down_proj, "mlp", 1)]
    fetched = fetch_prefix(key_value_pages, page_holder, page_slot)
    starts = [
        (place ^ j) * owned + chunk * rows
        for core in range(2)
        for chunk in range(CHUNKS)
        for j in range(core, members, 2)
    ]

    def picked(array):
        return jnp.concatenate([lax.dynamic_slice_in_dim(array, s, rows, 0) for s in starts], 0)

    places = jnp.concatenate([s + jnp.arange(rows) for s in starts], 0)
    asked, fetched, gates, uppers, downs = lax.optimization_barrier(
        (picked(queries), fetched, gates, uppers, downs)
    )
    kept, sent_rows = attend(
        asked,
        places,
        picked(segment_ids),
        leaf_keys,
        leaf_token_values,
        fetched,
        segment_ids,
        req_parent[0],
        mid_parent[0],
        node_len[0],
        out_proj,
    )
    span = members // 2 * rows
    streams, mixed = [], []
    for chunk in range(CHUNKS):
        own = lax.dynamic_slice_in_dim(residual, place * owned + chunk * rows, rows, 0)
        part = slice(chunk * span, (chunk + 1) * span)
        summed = sum_heads(kept[part], sent_rows[part], rows)
        streams.append((own.astype(jnp.float32) + summed).astype(jnp.bfloat16))
    for chunk in range(CHUNKS):
        tokens = gather_tokens(rms_norm(streams[chunk], norm_gain))
        mixed.append(feed_forward(tokens, gates, uppers, downs))
    layer_rows, next_rows, sent = [], [], []
    for chunk in range(CHUNKS):
        summed, sides = scatter_sum(mixed[chunk], rows)
        sent.append(sides)
        layer = (streams[chunk].astype(jnp.float32) + summed).astype(jnp.bfloat16)
        layer_rows.append(layer)
        next_rows.append(gather_heads(rms_norm(layer, next_gain)))
    layer_out = jnp.concatenate(layer_rows, 0)
    held = hold(lax.optimization_barrier((qkv_proj, sent))[0])
    next_normed = jnp.concatenate(
        [next_rows[c][j] for j in range(members) for c in range(CHUNKS)], 0
    )
    qkv_out = (
        jnp.dot(next_normed, held, preferred_element_type=jnp.float32) + qkv_bias
    ).astype(jnp.bfloat16)
    return (layer_out, qkv_out)


def solution(mesh):
    placed = (
        P("req", "mlp"),
        P("req", "mlp"),
        P("req", "mlp"),
        P("req", None, None, "mlp"),
        P(),
        P(),
        P("req"),
        P("req", None),
        P("req", None),
        P("req", None),
        P("req", None),
        P("mlp", None),
        P(),
        P(None, ("req", "mlp")),
        P(None, ("req", "mlp")),
        P(("req", "mlp"), None),
        P(),
        P(None, "mlp"),
        P("mlp"),
    )
    return jax.shard_map(
        body,
        mesh=mesh,
        in_specs=placed,
        out_specs=(P(("req", "mlp"), None), P("req", "mlp")),
        check_vma=False,
    )
```

```python
import math

import jax
import jax.numpy as jnp
from jax import lax
from jax.experimental import pallas as pl
from jax.experimental.pallas import tpu as pltpu
from jax.sharding import PartitionSpec as P

HEAD_SIZE = 128
QUERY_PER_KV = 5
REQ_DEV = 8
ROOT_DEV = 2
MID_DEV = 4
NODES_DEV = 6
NODE_MAX = 256
OUTER = 4
CHUNKS = 2


EPS = 1e-06


def rms_norm(stream, gain):
    values = stream.astype(jnp.float32)
    mean_sq = jnp.mean(values * values, axis=-1, keepdims=True)
    return (values * lax.rsqrt(mean_sq + EPS) * gain).astype(jnp.bfloat16)


def swap(array, axis, step):
    return lax.ppermute(array, axis, [(i, i ^ step) for i in range(lax.axis_size(axis))])


def attend_kernel(
    local_ref,
    entry_ref,
    queries_ref,
    limits_ref,
    query_segments_ref,
    places_ref,
    segments_ref,
    own_pages_ref,
    sent_pages_ref,
    leaf_keys_ref,
    leaf_values_ref,
    proj_ref,
    kept_ref,
    sent_ref,
    keys,
    values,
    mask,
    heads_out,
    proj,
    proj_sem,
):
    fetch = pltpu.make_async_copy(proj_ref, proj, proj_sem)
    fetch.start()
    tokens = queries_ref.shape[0]
    page = own_pages_ref.shape[2]
    pages = own_pages_ref.shape[0]
    prefix = pages * page
    node_tokens = prefix // NODES_DEV
    leaf_tokens = leaf_keys_ref.shape[0]
    heads_kv = leaf_keys_ref.shape[1] // HEAD_SIZE
    for p in range(pages):
        span = pl.ds(p * page, page)

        @pl.when(local_ref[p] == 1)
        def _():
            keys[span] = own_pages_ref[p, 0]
            values[span] = own_pages_ref[p, 1]

        @pl.when(local_ref[p] == 0)
        def _():
            keys[span] = sent_pages_ref[entry_ref[p], 0]
            values[span] = sent_pages_ref[entry_ref[p], 1]

    keys[pl.ds(prefix, leaf_tokens)] = leaf_keys_ref[...]
    values[pl.ds(prefix, leaf_tokens)] = leaf_values_ref[...]
    at = lax.broadcasted_iota(jnp.int32, (tokens, node_tokens), 1)
    for n in range(NODES_DEV):
        seen = at < limits_ref[:, n : n + 1]
        mask[:, n * node_tokens : (n + 1) * node_tokens] = jnp.where(seen, 0.0, -1e30)
    at = lax.broadcasted_iota(jnp.int32, (tokens, leaf_tokens), 1)
    seen = (segments_ref[...] == query_segments_ref[...]) & (at <= places_ref[...])
    mask[:, prefix:] = jnp.where(seen, 0.0, -1e30)
    scale = 1.0 / math.sqrt(HEAD_SIZE)
    for g in range(heads_kv):
        group = pl.ds(g * HEAD_SIZE, HEAD_SIZE)
        heads = [pl.ds((g * QUERY_PER_KV + h) * HEAD_SIZE, HEAD_SIZE) for h in range(QUERY_PER_KV)]
        score = lax.dot_general(
            jnp.concatenate([queries_ref[:, head] for head in heads], 0),
            keys[:, group],
            (((1,), (1,)), ((), ())),
            preferred_element_type=jnp.float32,
        )
        score = score.reshape(QUERY_PER_KV, tokens, -1) * scale + mask[...][None]
        top = jnp.max(score, axis=2, keepdims=True)
        expo = jnp.exp(score - top)
        total = jnp.sum(expo, axis=2, keepdims=True)
        summed = jnp.dot(
            expo.astype(jnp.bfloat16).reshape(QUERY_PER_KV * tokens, -1),
            values[:, group],
            preferred_element_type=jnp.float32,
        )
        result = (summed.reshape(QUERY_PER_KV, tokens, -1) / total).astype(jnp.bfloat16)
        for h, head in enumerate(heads):
            heads_out[:, head] = result[h]
    fetch.wait()
    half = tokens // 2
    span = kept_ref.shape[1] // 4
    for n in range(4):
        part = pl.ds(n * span, span)
        product = jnp.dot(heads_out[...], proj[:, part], preferred_element_type=jnp.float32)
        kept_ref[:, part] = product[:half]
        sent_ref[:, part] = product[half:].astype(jnp.bfloat16)


def attend(
    queries,
    places,
    query_segments,
    leaf_keys,
    leaf_values,
    fetched,
    segments,
    parents,
    roots,
    lengths,
    out_proj,
):
    is_local, entry, own_pages, sent_pages = fetched
    tokens, leaf_tokens = queries.shape[0], leaf_keys.shape[0]
    middle = jnp.sum(
        (query_segments[:, None] == jnp.arange(REQ_DEV)[None, :]) * parents[None, :], axis=1
    )
    root = jnp.sum((middle[:, None] == jnp.arange(MID_DEV)[None, :]) * roots[None, :], axis=1)
    node = jnp.arange(NODES_DEV)[None, :]
    on_path = (node == root[:, None]) | (node == ROOT_DEV + middle[:, None])
    limits = jnp.where(on_path, lengths[None, :], 0)
    key_count = NODES_DEV * NODE_MAX + leaf_tokens
    scalars = pl.BlockSpec(memory_space=pltpu.SMEM)
    whole = pl.BlockSpec(memory_space=pltpu.VMEM)
    columns = leaf_keys.shape[1]
    heads = queries.shape[1] // HEAD_SIZE
    return pl.pallas_call(
        attend_kernel,
        in_specs=[scalars] * 2 + [whole] * 9 + [pl.BlockSpec(memory_space=pltpu.HBM)],
        out_specs=[whole, whole],
        out_shape=[
            jax.ShapeDtypeStruct((tokens // 2, out_proj.shape[1]), jnp.float32),
            jax.ShapeDtypeStruct((tokens // 2, out_proj.shape[1]), jnp.bfloat16),
        ],
        scratch_shapes=[
            pltpu.VMEM((key_count, columns), jnp.bfloat16),
            pltpu.VMEM((key_count, columns), jnp.bfloat16),
            pltpu.VMEM((tokens, key_count), jnp.float32),
            pltpu.VMEM(queries.shape, jnp.bfloat16),
            pltpu.VMEM(out_proj.shape, jnp.bfloat16),
            pltpu.SemaphoreType.DMA(()),
        ],
        compiler_params=pltpu.CompilerParams(vmem_limit_bytes=51 * 1024 * 1024),
        cost_estimate=pl.CostEstimate(
            flops=4 * tokens * heads * HEAD_SIZE * key_count + 2 * tokens * out_proj.size,
            bytes_accessed=8 * key_count * columns + 2 * out_proj.size,
            transcendentals=tokens * heads * key_count,
        ),
        name="attend",
    )(
        is_local,
        entry,
        queries,
        limits,
        query_segments[:, None],
        places[:, None],
        segments[None, :],
        own_pages,
        sent_pages,
        leaf_keys,
        leaf_values,
        out_proj,
    )


def fetch_prefix(key_value_pages, page_holder, page_slot):
    groups = lax.axis_size("req")
    myself = lax.axis_index("req")
    holders = page_holder.reshape(groups, -1)
    slots = page_slot.reshape(groups, -1)
    token_count = holders.shape[1]
    room = (token_count // 2 + groups - 2) // (groups - 1)
    earlier = jnp.arange(token_count)[None, :] < jnp.arange(token_count)[:, None]
    same = holders[:, :, None] == holders[:, None, :]
    rank = jnp.sum(same & earlier[None, :, :], axis=-1)
    count = page_holder.shape[2]
    index = jnp.arange(page_holder.shape[1])[:, None] * count + jnp.arange(count)[None, :]
    asked = (page_holder == myself) & (jnp.arange(groups)[:, None, None] != myself)
    ends = [jnp.min(jnp.where(asked, index, token_count), axis=(1, 2))]
    if room > 1:
        ends.append(jnp.max(jnp.where(asked, index, -1), axis=(1, 2)))
    send_slot = jnp.stack(
        [jnp.sum(jnp.where(index == end[:, None, None], page_slot, 0), axis=(1, 2)) for end in ends],
        1,
    )
    outgoing = jnp.swapaxes(key_value_pages[send_slot.reshape(-1)], 1, 2)
    incoming = lax.all_to_all(outgoing, "req", split_axis=0, concat_axis=0, tiled=True)
    own_holders = lax.dynamic_index_in_dim(holders, myself, 0, keepdims=False)
    own_slots = lax.dynamic_index_in_dim(slots, myself, 0, keepdims=False)
    own_rank = lax.dynamic_index_in_dim(rank, myself, 0, keepdims=False)
    entry = own_holders * room + jnp.minimum(own_rank, room - 1)
    local = jnp.swapaxes(key_value_pages[own_slots], 1, 2)
    return (own_holders == myself).astype(jnp.int32), entry, local, incoming


def gather_tokens(rows):
    inner = lax.axis_size("req") // OUTER
    across = lax.axis_size("mlp") // 2
    column = jnp.concatenate(
        [rows] + [swap(rows, "req", k * inner) for k in range(1, OUTER)], 0
    )
    half = column.shape[0] // 2
    by_x = {k: swap(column, "mlp", 2 * k) for k in range(1, across)}
    by_y = {l: swap(column, "req", l) for l in range(1, inner)}
    blocks = [column] + list(by_x.values()) + list(by_y.values())
    for k in range(1, across):
        for l in range(1, inner):
            blocks.append(swap(by_y[l][:half], "mlp", 2 * k))
            blocks.append(swap(by_x[k][half:], "req", l))
    return jnp.concatenate(blocks, 0)


def scatter_sum(partial, rows):
    inner = lax.axis_size("req") // OUTER
    across = lax.axis_size("mlp") // 2
    size = OUTER * rows
    half = size // 2
    blocks = [partial[i * size : (i + 1) * size] for i in range(across * inner)]
    wide = jnp.float32
    column = blocks[0].astype(wide)
    by_x = {k: blocks[k].astype(wide) for k in range(1, across)}
    by_y = {l: blocks[across - 1 + l].astype(wide) for l in range(1, inner)}
    at = across + inner - 1
    for k in range(1, across):
        for l in range(1, inner):
            first = swap(blocks[at][:half], "mlp", 2 * k).astype(wide)
            second = swap(blocks[at][half:], "req", l).astype(wide)
            by_y[l] = jnp.concatenate([by_y[l][:half] + first, by_y[l][half:]], 0)
            by_x[k] = jnp.concatenate([by_x[k][:half], by_x[k][half:] + second], 0)
            at += 1
    by_x = {k: part.astype(jnp.bfloat16) for k, part in by_x.items()}
    by_y = {l: part.astype(jnp.bfloat16) for l, part in by_y.items()}
    for k in range(1, across):
        column = column + swap(by_x[k], "mlp", 2 * k).astype(wide)
    for l in range(1, inner):
        column = column + swap(by_y[l], "req", l).astype(wide)
    total = column[:rows]
    for k in range(1, OUTER):
        part = column[k * rows : (k + 1) * rows].astype(jnp.bfloat16)
        total = total + swap(part, "req", k * inner).astype(wide)
    return total, (by_x, by_y)


def sum_heads(kept, sent, rows):
    wide = jnp.float32
    even = kept + swap(sent, "mlp", 1).astype(wide)
    total = even[:rows]
    for k in range(1, kept.shape[0] // rows):
        part = even[k * rows : (k + 1) * rows].astype(jnp.bfloat16)
        total = total + swap(part, "mlp", 2 * k).astype(wide)
    return total


def gather_heads(rows):
    members = lax.axis_size("mlp")
    place = lax.axis_index("mlp")
    size = rows.shape[0]
    near = [rows] + [swap(rows, "mlp", 2 * k) for k in range(1, members // 2)]
    far = swap(jnp.concatenate(near, 0), "mlp", 1)
    blocks = []
    for k, block in enumerate(near):
        blocks += [block, far[k * size : (k + 1) * size]]
    step = 1
    while step < members:
        flip = (place // step) % 2 == 1
        blocks = [
            jnp.where(flip, blocks[j ^ step], blocks[j]) for j in range(members)
        ]
        step *= 2
    return blocks


def feed_forward_kernel(x_ref, g0, g1, u0, u1, d0, d1, out_ref, wide_rows, down_rows, hidden, sems):
    sources = [g0, u0, g1, u1, d0, d1]
    targets = [wide_rows.at[n] for n in range(4)] + [down_rows.at[n] for n in range(2)]
    copies = [
        pltpu.make_async_copy(source, target, sems.at[n])
        for n, (source, target) in enumerate(zip(sources, targets))
    ]
    for copy in copies:
        copy.start()
    flip = (((1,), (1,)), ((), ()))
    for n in range(2):
        copies[2 * n].wait()
        gate = lax.dot_general(
            x_ref[...], wide_rows[2 * n], flip, preferred_element_type=jnp.float32
        )
        copies[2 * n + 1].wait()
        upper = lax.dot_general(
            x_ref[...], wide_rows[2 * n + 1], flip, preferred_element_type=jnp.float32
        )
        hidden[n] = (gate / (1.0 + jnp.exp(-gate)) * upper).astype(jnp.bfloat16)
    copies[4].wait()
    copies[5].wait()
    span = out_ref.shape[1] // 4
    for n in range(4):
        part = pl.ds(n * span, span)
        total = jnp.dot(hidden[0], down_rows[0, :, part], preferred_element_type=jnp.float32)
        total += jnp.dot(hidden[1], down_rows[1, :, part], preferred_element_type=jnp.float32)
        out_ref[:, part] = total.astype(jnp.bfloat16)


def feed_forward(tokens, gates, uppers, downs):
    rows, width = tokens.shape
    units = gates[0].shape[0]
    far = pl.BlockSpec(memory_space=pltpu.HBM)
    near = pl.BlockSpec(memory_space=pltpu.VMEM)
    return pl.pallas_call(
        feed_forward_kernel,
        in_specs=[near] + [far] * 6,
        out_specs=near,
        out_shape=jax.ShapeDtypeStruct((rows, width), jnp.bfloat16),
        scratch_shapes=[
            pltpu.VMEM((4, units, width), jnp.bfloat16),
            pltpu.VMEM((2, units, width), jnp.bfloat16),
            pltpu.VMEM((2, rows, units), jnp.bfloat16),
            pltpu.SemaphoreType.DMA((6,)),
        ],
        compiler_params=pltpu.CompilerParams(vmem_limit_bytes=40 * 1024 * 1024),
        cost_estimate=pl.CostEstimate(
            flops=12 * rows * width * units,
            bytes_accessed=12 * width * units + 4 * rows * width,
            transcendentals=2 * rows * units,
        ),
        name="feed_forward",
    )(tokens, *gates, *uppers, *downs)


def hold_kernel(source_ref, out_ref, sem):
    copy = pltpu.make_async_copy(source_ref, out_ref, sem)
    copy.start()
    copy.wait()


def hold(array):
    return pl.pallas_call(
        hold_kernel,
        in_specs=[pl.BlockSpec(memory_space=pltpu.HBM)],
        out_specs=pl.BlockSpec(memory_space=pltpu.VMEM),
        out_shape=pltpu.VMEM(array.shape, array.dtype),
        scratch_shapes=[pltpu.SemaphoreType.DMA(())],
        compiler_params=pltpu.CompilerParams(vmem_limit_bytes=2 * 1024 * 1024),
        cost_estimate=pl.CostEstimate(
            flops=0, bytes_accessed=4 * array.size, transcendentals=0
        ),
        name="hold",
    )(array)


def body(
    queries,
    leaf_keys,
    leaf_token_values,
    key_value_pages,
    page_holder,
    page_slot,
    segment_ids,
    req_parent,
    mid_parent,
    node_len,
    residual,
    out_proj,
    norm_gain,
    gate_proj,
    up_proj,
    down_proj,
    next_gain,
    qkv_proj,
    qkv_bias,
):
    group_tokens = queries.shape[0]
    members = lax.axis_size("mlp")
    place = lax.axis_index("mlp")
    owned = group_tokens // members
    rows = owned // CHUNKS
    gate_rows, up_rows = gate_proj.T, up_proj.T
    gates = [gate_rows, swap(gate_rows, "mlp", 1)]
    uppers = [up_rows, swap(up_rows, "mlp", 1)]
    downs = [down_proj, swap(down_proj, "mlp", 1)]
    fetched = fetch_prefix(key_value_pages, page_holder, page_slot)
    starts = [
        (place ^ j) * owned + chunk * rows
        for core in range(2)
        for chunk in range(CHUNKS)
        for j in range(core, members, 2)
    ]

    def picked(array):
        return jnp.concatenate([lax.dynamic_slice_in_dim(array, s, rows, 0) for s in starts], 0)

    places = jnp.concatenate([s + jnp.arange(rows) for s in starts], 0)
    asked, fetched, gates, uppers, downs = lax.optimization_barrier(
        (picked(queries), fetched, gates, uppers, downs)
    )
    kept, sent_rows = attend(
        asked,
        places,
        picked(segment_ids),
        leaf_keys,
        leaf_token_values,
        fetched,
        segment_ids,
        req_parent[0],
        mid_parent[0],
        node_len[0],
        out_proj,
    )
    span = members // 2 * rows
    streams, mixed = [], []
    for chunk in range(CHUNKS):
        own = lax.dynamic_slice_in_dim(residual, place * owned + chunk * rows, rows, 0)
        part = slice(chunk * span, (chunk + 1) * span)
        summed = sum_heads(kept[part], sent_rows[part], rows)
        streams.append((own.astype(jnp.float32) + summed).astype(jnp.bfloat16))
    for chunk in range(CHUNKS):
        tokens = gather_tokens(rms_norm(streams[chunk], norm_gain))
        mixed.append(feed_forward(tokens, gates, uppers, downs))
    layer_rows, next_rows, sent = [], [], []
    for chunk in range(CHUNKS):
        summed, sides = scatter_sum(mixed[chunk], rows)
        sent.append(sides)
        layer = (streams[chunk].astype(jnp.float32) + summed).astype(jnp.bfloat16)
        layer_rows.append(layer)
        next_rows.append(gather_heads(rms_norm(layer, next_gain)))
    layer_out = jnp.concatenate(layer_rows, 0)
    held = hold(lax.optimization_barrier((qkv_proj, sent))[0])
    next_normed = jnp.concatenate(
        [next_rows[c][j] for j in range(members) for c in range(CHUNKS)], 0
    )
    qkv_out = (
        jnp.dot(next_normed, held, preferred_element_type=jnp.float32) + qkv_bias
    ).astype(jnp.bfloat16)
    return (layer_out, qkv_out)


def solution(mesh):
    placed = (
        P("req", "mlp"),
        P("req", "mlp"),
        P("req", "mlp"),
        P("req", None, None, "mlp"),
        P(),
        P(),
        P("req"),
        P("req", None),
        P("req", None),
        P("req", None),
        P("req", None),
        P("mlp", None),
        P(),
        P(None, ("req", "mlp")),
        P(None, ("req", "mlp")),
        P(("req", "mlp"), None),
        P(),
        P(None, "mlp"),
        P("mlp"),
    )
    return jax.shard_map(
        body,
        mesh=mesh,
        in_specs=placed,
        out_specs=(P(("req", "mlp"), None), P("req", "mlp")),
        check_vma=False,
    )
```
